512 devices in a mesh: dp: 64 (over x, y, z_lo), section: 8 (over z_hi, core).
Axes of the slice: x: 4, y: 4, z: 16 (z_hi: 4, z_lo: 4; z = z_hi * 4 + z_lo), core: 2. Of those that a mesh axis runs over, the one named last changes fastest.
Arguments:
- latents: bfloat16 [64, 4, 8, 8, 256], P('dp'), may hold values from -6 to 6
- cotangent: bfloat16 [64, 4, 8, 8, 256], P('dp'), may hold values from -0.046875 to 0.046875
- spatial_weight: bfloat16 [8, 2304, 256], P('section'), may hold values from -0.125 to 0.125
- temporal_weight: bfloat16 [8, 768, 256], P('section'), may hold values from -0.21875 to 0.21875
- norm_gain: float32 [8, 256], P('section'), may hold values from 0.25 to 1.75
- norm_shift: float32 [8, 256], P('section'), may hold values from -3 to 3
Outputs:
- spatial_grad: float32 [8, 2304, 256], P('section', 'dp')
- temporal_grad: float32 [8, 768, 256], P('section', 'dp')
- norm_grad: float32 [8, 2, 256], P('section')
The draws below stay inside these ranges and needn't reach their ends.
All inputs are finite; a program needn't handle non-finite values.
Results may differ from the reference program's by a relative error of at most 0.015.
Values may be sent and summed in bfloat16 or wider, within the bound.
A program may use at most 64 MiB of HBM per device.

```python
import jax
import jax.numpy as jnp
from jax import lax

C = 256
GROUPS = 32
FR = 4
HS = 8
WS = 8
MB = 1
BATCH = 64
N_DP = 64
N_SECTION = 8


def block_levels(own_key, extent, cuts, low, high):
    def one(position, shards_of):
        heights = jax.random.uniform(jax.random.fold_in(jax.random.fold_in(own_key, 6), position), (shards_of,), jnp.float32, low / len(cuts), high / len(cuts))
        return jnp.repeat(jnp.exp(heights), extent[position] // shards_of).reshape((-1,) + (1,) * (len(extent) - position - 1))

    factor_of = one(*cuts[0])
    for cut in cuts[1:]:
        factor_of = factor_of * one(*cut)
    return factor_of


def scatter_about(stream_key, dims, width, limit, cuts=(), kind=jnp.bfloat16):
    level = block_levels(stream_key, dims, cuts, -0.22, 0.18) if cuts else 1.0
    array = jax.random.normal(stream_key, dims, jnp.float32) * width * level
    return jnp.minimum(jnp.maximum(array, -limit), limit).astype(kind)


def setup_inputs(seed: int = 0) -> dict:
    key_list = jax.random.split(jax.random.key(seed), 7)
    latents = scatter_about(key_list[0], (BATCH, FR, HS, WS, C), 1.0, 6.0, ((0, 64),))
    cotangent = scatter_about(key_list[1], (BATCH, FR, HS, WS, C), ((N_DP * MB * FR * HS * WS) ** -0.5), 0.046875, ((0, 64),))
    spatial_weight = scatter_about(key_list[2], (N_SECTION, 9 * C, C), (9 * C) ** -0.5, 0.125, ((0, 8),))
    temporal_weight = scatter_about(key_list[3], (N_SECTION, 3 * C, C), (3 * C) ** -0.5, 0.21875, ((0, 8),))
    norm_gain = jnp.clip(1.0 + 0.15 * jax.random.normal(key_list[4], (N_SECTION, C), jnp.float32), 0.25, 1.75)
    norm_shift = scatter_about(key_list[5], (N_SECTION, C), 0.5, 3.0, ((0, 8),), jnp.float32)
    return dict(latents=latents, cotangent=cotangent, spatial_weight=spatial_weight, temporal_weight=temporal_weight, norm_gain=norm_gain, norm_shift=norm_shift)


epsilon = 1e-05
spatial_offsets = ((0, -1, -1), (0, -1, 0), (0, -1, 1), (0, 0, -1), (0, 0, 0), (0, 0, 1), (0, 1, -1), (0, 1, 0), (0, 1, 1))
temporal_offsets = ((-1, 0, 0), (0, 0, 0), (1, 0, 0))

def shifted(field, offset):
    frames, height, columns, channels = field.shape
    padded = jnp.pad(field, ((1, 1), (1, 1), (1, 1), (0, 0)))
    return padded[1 + offset[0]:1 + offset[0] + frames, 1 + offset[1]:1 + offset[1] + height, 1 + offset[2]:1 + offset[2] + columns, :]

def stacked(field, offsets, sign):
    parts = [shifted(field, (sign * offset[0], sign * offset[1], sign * offset[2])) for offset in offsets]
    joined = jnp.concatenate(parts, axis=3)
    return joined.reshape(-1, joined.shape[3])

def contract_rows(left, right):
    return lax.dot_general(left, right, (((0,), (0,)), ((), ())), preferred_element_type=jnp.float32)

def apply_back(columns_in, weight, taps):
    rows = columns_in.shape[0]
    channels = weight.shape[1]
    return lax.dot_general(columns_in.reshape(rows, taps, channels), weight.reshape(taps, channels, channels), (((1, 2), (0, 2)), ((), ())), preferred_element_type=jnp.float32)

def section_parts(inputs, spatial, temporal, gain, shift):
    frames, height, columns, channels = inputs.shape
    rows = frames * height * columns
    grouped = inputs.reshape(rows, GROUPS, channels // GROUPS)
    center = lax.optimization_barrier(jnp.mean(grouped, axis=(0, 2), keepdims=True))
    deviation = grouped - center
    variance = lax.optimization_barrier(jnp.mean(deviation * deviation, axis=(0, 2), keepdims=True))
    scaling = lax.rsqrt(variance + epsilon)
    normed = (deviation * scaling).reshape(rows, channels)
    before = normed * gain + shift
    active = (before * jax.nn.sigmoid(before)).astype(jnp.bfloat16).reshape(inputs.shape)
    middle = jnp.dot(stacked(active, spatial_offsets, 1), spatial, preferred_element_type=jnp.float32).astype(jnp.bfloat16).reshape(inputs.shape)
    branch = jnp.dot(stacked(middle, temporal_offsets, 1), temporal, preferred_element_type=jnp.float32)
    output = (inputs.reshape(rows, channels) + branch).astype(jnp.bfloat16).reshape(inputs.shape)
    return (output, normed, before, active, middle, scaling)

def section_backward(inputs, upstream, spatial, temporal, gain, shift):
    output, normed, before, active, middle, scaling = section_parts(inputs, spatial, temporal, gain, shift)
    rows, channels = normed.shape
    flat_up = upstream.reshape(rows, channels)
    temporal_term = contract_rows(stacked(middle, temporal_offsets, 1), flat_up)
    middle_grad = apply_back(stacked(upstream, temporal_offsets, -1), temporal, 3).astype(jnp.bfloat16).reshape(upstream.shape)
    spatial_term = contract_rows(stacked(active, spatial_offsets, 1), middle_grad.reshape(rows, channels))
    active_grad = apply_back(stacked(middle_grad, spatial_offsets, -1), spatial, 9)
    sigma = jax.nn.sigmoid(before)
    before_grad = active_grad * sigma * (1.0 + before * (1.0 - sigma))
    gain_term = lax.optimization_barrier(jnp.sum(before_grad * normed, axis=0))
    shift_term = lax.optimization_barrier(jnp.sum(before_grad, axis=0))
    normed_grad = (before_grad * gain).reshape(rows, GROUPS, channels // GROUPS)
    grouped_normed = normed.reshape(rows, GROUPS, channels // GROUPS)
    inner = lax.optimization_barrier(jnp.mean(normed_grad, axis=(0, 2), keepdims=True))
    project = lax.optimization_barrier(jnp.mean(normed_grad * grouped_normed, axis=(0, 2), keepdims=True))
    input_grad = scaling * (normed_grad - inner - grouped_normed * project)
    total = (flat_up.astype(jnp.float32) + input_grad.reshape(rows, channels)).astype(jnp.bfloat16).reshape(upstream.shape)
    return (total, spatial_term, temporal_term, gain_term, shift_term)

def reference(latents, cotangent, spatial_weight, temporal_weight, norm_gain, norm_shift):
    midpoint = N_SECTION // 2

    def one_sample(carry, sample):
        latent_one, cotangent_one = sample
        arriving = latent_one
        skip_store = {}
        saved = []
        for section_id in range(N_SECTION):
            inputs = arriving.astype(jnp.float32)
            if section_id >= midpoint:
                inputs = inputs + skip_store[N_SECTION - 1 - section_id].astype(jnp.float32)
            saved.append(inputs)
            arriving = section_parts(inputs, spatial_weight[section_id], temporal_weight[section_id], norm_gain[section_id], norm_shift[section_id])[0]
            if section_id < midpoint:
                skip_store[section_id] = arriving
        returning = cotangent_one
        skip_grads = {}
        terms = [None] * N_SECTION
        for section_id in reversed(range(N_SECTION)):
            upstream = returning
            if section_id < midpoint:
                upstream = (returning.astype(jnp.float32) + skip_grads[section_id].astype(jnp.float32)).astype(jnp.bfloat16)
            result = section_backward(saved[section_id], upstream, spatial_weight[section_id], temporal_weight[section_id], norm_gain[section_id], norm_shift[section_id])
            returning = result[0]
            terms[section_id] = result[1:]
            if section_id >= midpoint:
                skip_grads[N_SECTION - 1 - section_id] = returning
        updated = tuple((carry[place] + jnp.stack([term[place] for term in terms]) for place in range(4)))
        return (updated, None)
    start = (jnp.zeros(spatial_weight.shape, jnp.float32), jnp.zeros(temporal_weight.shape, jnp.float32), jnp.zeros(norm_gain.shape, jnp.float32), jnp.zeros(norm_shift.shape, jnp.float32))
    totals, unused = lax.scan(one_sample, start, (latents, cotangent))
    return (totals[0], totals[1], jnp.stack([totals[2], totals[3]], axis=1))
```

```python
import functools

import jax
import jax.numpy as jnp
from jax import lax
from jax.experimental import pallas as pl
from jax.experimental.pallas import tpu as pltpu
from jax.sharding import PartitionSpec as P

MESH = pl.DeviceIdType.MESH
EPSILON = 1e-05
CELLS = 256
CH = 256
HALF = 128
SPATIAL = 2304
WEIGHT_ROWS = 3072
SLICE = WEIGHT_ROWS // 16
LONG = WEIGHT_ROWS // 4
SPATIAL_OFFSETS = tuple((dy, dx) for dy in (-1, 0, 1) for dx in (-1, 0, 1))
TEMPORAL_OFFSETS = (-1, 0, 1)
F32 = jnp.float32
BF16 = jnp.bfloat16


def group_mean(value):
    lane = lax.broadcasted_iota(jnp.int32, value.shape, 1)
    for step in (1, 2, 4):
        after = pltpu.roll(value, CH - step, axis=1)
        before = pltpu.roll(value, step, axis=1)
        value = value + jnp.where((lane & step) == 0, after, before)
    return value * 0.125


def over_groups(row_sum):
    wide = jnp.broadcast_to(row_sum * (1.0 / CELLS), (8, CH))
    return group_mean(wide)[0:1]


def shift_x(value, dx):
    if dx == 0:
        return value
    lines = value.reshape(32, 8, CH)
    moved = pltpu.roll(lines, (-dx) % 8, axis=1)
    column = lax.broadcasted_iota(jnp.int32, lines.shape, 1)
    inside = column != (7 if dx == 1 else 0)
    return jnp.where(inside, moved, 0.0).reshape(CELLS, CH)


def shift_y(value, dy):
    if dy == 0:
        return value
    frames = value.reshape(4, 64, CH)
    edge = jnp.zeros((4, 8, CH), value.dtype)
    if dy == 1:
        frames = jnp.concatenate([frames[:, 8:], edge], axis=1)
    else:
        frames = jnp.concatenate([edge, frames[:, :56]], axis=1)
    return frames.reshape(CELLS, CH)


def shift_t(value, dt):
    if dt == 0:
        return value
    edge = jnp.zeros((64, CH), value.dtype)
    if dt == 1:
        return jnp.concatenate([value[64:], edge], axis=0)
    return jnp.concatenate([edge, value[:192]], axis=0)


def fill_spatial(cols, value, sign):
    for dx in (-1, 0, 1):
        moved = shift_x(value, sign * dx)
        for dy in (-1, 0, 1):
            tap = SPATIAL_OFFSETS.index((dy, dx))
            cols[:, tap * CH : (tap + 1) * CH] = shift_y(moved, sign * dy).astype(BF16)


def fill_temporal(cols, value, sign):
    for tap, dt in enumerate(TEMPORAL_OFFSETS):
        cols[:, tap * CH : (tap + 1) * CH] = shift_t(value, sign * dt)


def times_transposed(left, right):
    return lax.dot_general(left, right, (((1,), (1,)), ((), ())), preferred_element_type=F32)


def kernel(
    latents, cotangent, gain_ref, shift_ref, spatial_ref, temporal_ref,
    spatial_out, temporal_out, norm_out,
    wall, prm, hist, ghist, normed_s, slope_s, scale_s, cols, tcols, act_t, mid_t,
    gsend, first_in, first_sum, second_in, third_f, third_out, third_in, norm_acc,
    local_sem, z_send, z_recv, mid_send, mid_recv, last_send, last_recv,
    core_send, core_recv, prm_send, prm_recv,
    g1_send, g1_recv, g2_send, g2_recv, g3_send, g3_recv, n_send, n_recv,
):
    dp = lax.axis_index("dp")
    pos = lax.axis_index("section")
    px = dp // 16
    py = (dp // 4) % 4
    pz = dp % 4
    block = pos // 2
    core = pos % 2

    def at_x(x):
        return (x * 16 + py * 4 + pz, pos)

    def at_y(y):
        return (px * 16 + y * 4 + pz, pos)

    def at_z(z):
        return (px * 16 + py * 4 + z, pos)

    def at_section(s):
        return (dp, s)

    def copy(src, dst, send, recv, device):
        return pltpu.make_async_remote_copy(
            src_ref=src, dst_ref=dst, send_sem=send, recv_sem=recv,
            device_id=device, device_id_type=MESH,
        )

    along = ((px, at_x), (py, at_y))

    loads = [
        pltpu.make_async_copy(spatial_ref.at[0], wall.at[pos, pl.ds(0, SPATIAL)], local_sem.at[0]),
        pltpu.make_async_copy(
            temporal_ref.at[0], wall.at[pos, pl.ds(SPATIAL, WEIGHT_ROWS - SPATIAL)], local_sem.at[1]
        ),
    ]
    for load in loads:
        load.start()

    barrier = pltpu.get_barrier_semaphore()
    for d in (1, 2, 3):
        for mine, place in along + ((pz, at_z),):
            pl.semaphore_signal(
                barrier, inc=1, device_id=place((mine + d) % 4), device_id_type=MESH
            )
    for d in range(1, 8):
        pl.semaphore_signal(
            barrier, inc=1, device_id=at_section((pos + d) % 8), device_id_type=MESH
        )

    rest = jnp.zeros((6, CH), F32)
    prm[pos] = jnp.concatenate([gain_ref[...], shift_ref[...], rest], axis=0)
    hist[0] = latents[...]
    ghist[8] = cotangent[...]
    for load in loads:
        load.wait()
    pl.semaphore_wait(barrier, 16)

    def prm_copy(d):
        return copy(
            prm.at[pos], prm.at[pos], prm_send.at[d], prm_recv.at[pos], at_section((pos + d) % 8)
        )

    def prm_arrival(d):
        other = (pos + d) % 8
        return copy(prm.at[other], prm.at[other], prm_send.at[d], prm_recv.at[other], at_section(other))

    for d in range(1, 8):
        prm_copy(d).start()

    def core_copy(pair):
        section = 2 * pair + core
        return copy(
            wall.at[section], wall.at[section], core_send.at[pair], core_recv.at[pair],
            at_section(block * 2 + 1 - core),
        )

    def core_arrival(pair):
        section = 2 * pair + 1 - core
        return copy(
            wall.at[section], wall.at[section], core_send.at[pair], core_recv.at[pair],
            at_section(block * 2 + 1 - core),
        )

    core_copy(block).start()

    def part(section, row, rows, half):
        return wall.at[section, pl.ds(row, rows), pl.ds(half * HALF, HALF)]

    slice_row = ((py * 4 + px) * SLICE, (px * 4 + py) * SLICE)
    long_row = (py * LONG, px * LONG)

    def z_copy(d, half):
        target = (block + d) % 4
        order = jnp.where(block < target, block, block - 1)
        ref = part(pos, slice_row[half], SLICE, half)
        return copy(
            ref, ref, z_send.at[d, half], z_recv.at[order, half], at_section(target * 2 + core)
        )

    for d in (1, 3, 2):
        for half in (0, 1):
            z_copy(d, half).start()

    def pair_of(k):
        return jnp.where(k < block, k, k + 1)

    def z_arrival(k, half):
        section = 2 * pair_of(k) + core
        ref = part(section, slice_row[half], SLICE, half)
        return copy(ref, ref, z_send.at[1, half], z_recv.at[k, half], at_section((pos + 2) % 8))

    def mid_copy(k, half, d):
        mine, place = along[half]
        ref = part(2 * pair_of(k) + core, slice_row[half], SLICE, half)
        return copy(
            ref, ref, mid_send.at[k, half, d], mid_recv.at[k, half, mine], place((mine + d) % 4)
        )

    def mid_arrival(k, half, d):
        mine, place = along[half]
        source = (mine + d) % 4
        row = long_row[half] + source * SLICE
        ref = part(2 * pair_of(k) + core, row, SLICE, half)
        return copy(ref, ref, mid_send.at[k, half, d], mid_recv.at[k, half, source], place(source))

    def last_copy(k, half, d):
        mine, place = along[1 - half]
        ref = part(2 * pair_of(k) + core, long_row[half], LONG, half)
        return copy(
            ref, ref, last_send.at[k, half, d], last_recv.at[k, half, mine], place((mine + d) % 4)
        )

    def last_arrival(k, half, d):
        mine, place = along[1 - half]
        source = (mine + d) % 4
        ref = part(2 * pair_of(k) + core, source * LONG, LONG, half)
        return copy(ref, ref, last_send.at[k, half, d], last_recv.at[k, half, source], place(source))

    def spread(k, carry):
        for half in (0, 1):
            z_arrival(k, half).wait_recv()
            for d in (1, 3, 2):
                mid_copy(k, half, d).start()
        for half in (0, 1):
            for d in (1, 3, 2):
                mid_arrival(k, half, d).wait_recv()
            for d in (1, 3, 2):
                last_copy(k, half, d).start()
        return carry

    def forward(s):
        params = prm[s]
        gain = params[0:1]
        shift = params[1:2]
        decoder = s >= 4
        skip = jnp.where(decoder, 1.0, 0.0)
        inputs = hist[s].astype(F32) + skip * hist[jnp.where(decoder, 8 - s, 0)].astype(F32)
        center = over_groups(jnp.sum(inputs, axis=0, keepdims=True))
        deviation = inputs - center
        variance = over_groups(jnp.sum(deviation * deviation, axis=0, keepdims=True))
        scaling = lax.rsqrt(variance + EPSILON)
        normed = deviation * scaling
        before = normed * gain + shift
        sigma = jax.nn.sigmoid(before)
        normed_s[s] = normed
        slope_s[s] = sigma * (1.0 + before * (1.0 - sigma))
        scale_s[s] = jnp.broadcast_to(scaling, (8, CH))

        @pl.when((s < 7) | (pos == 7))
        def _():
            active = before * sigma
            fill_spatial(cols, active, 1)
            middle = jnp.dot(cols[...], wall[s, 0:SPATIAL], preferred_element_type=F32)
            rounded = middle.astype(BF16)
            fill_temporal(tcols, rounded, 1)
            branch = jnp.dot(tcols[...], wall[s, SPATIAL:WEIGHT_ROWS], preferred_element_type=F32)
            hist[s + 1] = (inputs + branch).astype(BF16)

            @pl.when(s == pos)
            def _():
                act_t[...] = active.T.astype(BF16)
                mid_t[...] = middle.T.astype(BF16)

    def forward_pair(pair, carry):
        @pl.when(pair == jnp.where(block == 0, 1, 0))
        def _():
            lax.fori_loop(0, 3, spread, 0)

        @pl.when(pair != block)
        def _():
            k = jnp.where(pair < block, pair, pair - 1)
            for half in (0, 1):
                for d in (1, 3, 2):
                    last_arrival(k, half, d).wait_recv()
            core_copy(pair).start()

        @pl.when(pair == 0)
        def _():
            for d in range(1, 8):
                prm_arrival(d).wait_recv()

        core_arrival(pair).wait_recv()

        def one(index, inner):
            forward(2 * pair + index)
            return inner

        return lax.fori_loop(0, 2, one, carry)

    lax.fori_loop(0, 4, forward_pair, 0)

    def upstream(s):
        encoder = s < 4
        extra = jnp.where(encoder, 1.0, 0.0)
        other = ghist[jnp.where(encoder, 7 - s, 8)].astype(F32)
        return (ghist[s + 1].astype(F32) + extra * other).astype(BF16)

    def middle_grad(s, up):
        fill_temporal(tcols, up, -1)
        total = jnp.zeros((CELLS, CH), F32)
        for tap in range(3):
            weight = wall[s, SPATIAL + tap * CH : SPATIAL + (tap + 1) * CH]
            total = total + times_transposed(tcols[:, tap * CH : (tap + 1) * CH], weight)
        fill_spatial(cols, total, -1)

    def before_grad(s):
        total = jnp.zeros((CELLS, CH), F32)
        for tap in range(9):
            weight = wall[s, tap * CH : (tap + 1) * CH]
            total = total + times_transposed(cols[:, tap * CH : (tap + 1) * CH], weight)
        return total * slope_s[s]

    def backward(i, carry):
        s = 7 - i
        gain = prm[s][0:1]
        up = upstream(s)
        middle_grad(s, up)
        grad = before_grad(s)
        normed = normed_s[s]
        inner = over_groups(gain * jnp.sum(grad, axis=0, keepdims=True))
        project = over_groups(gain * jnp.sum(grad * normed, axis=0, keepdims=True))
        input_grad = scale_s[s][0:1] * (grad * gain - inner - normed * project)
        ghist[s] = (up.astype(F32) + input_grad).astype(BF16)
        return carry

    lax.fori_loop(0, 7 - pos, backward, 0)

    def store_rows(tile, row, per_x, per_y, base):
        end = row + CH
        while row < end:
            stop = min(end, (row // per_y + 1) * per_y)
            where_x = row // per_x
            where_y = (row % per_x) // per_y
            inside = row % per_y
            start = CH - (end - row)
            gsend[where_x, where_y, base + inside : base + inside + stop - row, :] = tile[
                start : start + stop - row
            ]
            row = stop

    up = upstream(pos)
    middle_grad(pos, up)
    for tap in range(3):
        tile = jnp.dot(mid_t[...], tcols[:, tap * CH : (tap + 1) * CH], preferred_element_type=F32)
        store_rows(tile.astype(BF16), tap * CH, 192, 48, 144)
    for tap in range(9):
        tile = jnp.dot(act_t[...], cols[:, tap * CH : (tap + 1) * CH], preferred_element_type=F32)
        store_rows(tile.astype(BF16), tap * CH, 576, 144, 0)

    def own_part(half, index):
        if half == 0:
            return gsend.at[index, :, :, pl.ds(0, HALF)]
        return gsend.at[:, index, :, pl.ds(HALF, HALF)]

    def g1_copy(half, d):
        mine, place = along[half]
        target = (mine + d) % 4
        return copy(
            own_part(half, target), first_in.at[half, mine], g1_send.at[half, d],
            g1_recv.at[half, mine], place(target),
        )

    def g1_arrival(half, d):
        mine, place = along[half]
        source = (mine + d) % 4
        return copy(
            own_part(half, source), first_in.at[half, source], g1_send.at[half, d],
            g1_recv.at[half, source], place(source),
        )

    def g2_copy(half, d):
        mine, place = along[1 - half]
        target = (mine + d) % 4
        return copy(
            first_sum.at[half, target], second_in.at[half, mine], g2_send.at[half, d],
            g2_recv.at[half, mine], place(target),
        )

    def g2_arrival(half, d):
        mine, place = along[1 - half]
        source = (mine + d) % 4
        return copy(
            first_sum.at[half, source], second_in.at[half, source], g2_send.at[half, d],
            g2_recv.at[half, source], place(source),
        )

    def g3_copy(d):
        target = (pz + d) % 4
        return copy(
            third_out.at[target], third_in.at[pz], g3_send.at[d], g3_recv.at[pz], at_z(target)
        )

    def g3_arrival(d):
        source = (pz + d) % 4
        return copy(
            third_out.at[source], third_in.at[source], g3_send.at[d], g3_recv.at[source], at_z(source)
        )

    for half in (0, 1):
        for d in (1, 3, 2):
            g1_copy(half, d).start()

    axes = along + ((pz, at_z),)

    def n_copy(phase, d):
        mine, place = axes[phase]
        return copy(
            norm_acc.at[phase, mine], norm_acc.at[phase, mine], n_send.at[phase, d],
            n_recv.at[phase, mine], place((mine + d) % 4),
        )

    def n_arrival(phase, d):
        mine, place = axes[phase]
        source = (mine + d) % 4
        return copy(
            norm_acc.at[phase, source], norm_acc.at[phase, source], n_send.at[phase, d],
            n_recv.at[phase, source], place(source),
        )

    grad = before_grad(pos)
    gain_term = jnp.sum(grad * normed_s[pos], axis=0, keepdims=True)
    shift_term = jnp.sum(grad, axis=0, keepdims=True)
    norm_value = jnp.concatenate([gain_term, shift_term, rest], axis=0)

    def norm_start(phase, value):
        norm_acc[phase, axes[phase][0]] = value
        for d in (1, 3, 2):
            n_copy(phase, d).start()

    def norm_finish(phase):
        for d in (1, 3, 2):
            n_arrival(phase, d).wait_recv()
        return ((norm_acc[phase, 0] + norm_acc[phase, 1]) + norm_acc[phase, 2]) + norm_acc[phase, 3]

    norm_start(0, norm_value)

    for half in (0, 1):
        mine = along[half][0]
        for d in (1, 3, 2):
            g1_arrival(half, d).wait_recv()
        for index in range(4):
            if half == 0:
                total = gsend[mine, index, :, 0:HALF].astype(F32)
            else:
                total = gsend[index, mine, :, HALF:CH].astype(F32)
            for d in (1, 2, 3):
                total = total + first_in[half, (mine + d) % 4, index].astype(F32)
            first_sum[half, index] = total.astype(BF16)
        for d in (1, 3, 2):
            g2_copy(half, d).start()

    norm_start(1, norm_finish(0))

    for half in (0, 1):
        mine = along[1 - half][0]
        for d in (1, 3, 2):
            g2_arrival(half, d).wait_recv()
        total = first_sum[half, mine].astype(F32)
        for d in (1, 2, 3):
            total = total + second_in[half, (mine + d) % 4].astype(F32)
        columns = slice(half * HALF, (half + 1) * HALF)
        for z in range(4):
            third_f[z, 0:36, columns] = total[z * 36 : (z + 1) * 36]
            third_f[z, 36:48, columns] = total[144 + z * 12 : 144 + (z + 1) * 12]
    for z in range(4):
        third_out[z] = third_f[z].astype(BF16)
    for d in (1, 3, 2):
        g3_copy(d).start()

    norm_start(2, norm_finish(1))

    total = third_f[pz]
    for d in (1, 3, 2):
        g3_arrival(d).wait_recv()
    for d in (1, 2, 3):
        total = total + third_in[(pz + d) % 4].astype(F32)
    spatial_out[0] = total[0:36]
    temporal_out[0] = total[36:48]
    norm_out[0] = norm_finish(2)[0:2]

    for d in range(1, 8):
        prm_copy(d).wait_send()
    for d in (1, 3, 2):
        for half in (0, 1):
            z_copy(d, half).wait_send()
            g1_copy(half, d).wait_send()
            g2_copy(half, d).wait_send()
        g3_copy(d).wait_send()
        for phase in range(3):
            n_copy(phase, d).wait_send()
    for k in range(3):
        for half in (0, 1):
            for d in (1, 3, 2):
                mid_copy(k, half, d).wait_send()
                last_copy(k, half, d).wait_send()
    for pair in range(4):
        core_copy(pair).wait_send()


def shards(latents, cotangent, spatial_weight, temporal_weight, norm_gain, norm_shift):
    vmem = pl.BlockSpec(memory_space=pltpu.VMEM)
    anywhere = pl.BlockSpec(memory_space=pl.ANY)
    dma = pltpu.SemaphoreType.DMA
    return pl.pallas_call(
        kernel,
        out_shape=(
            jax.ShapeDtypeStruct((1, 36, CH), F32),
            jax.ShapeDtypeStruct((1, 12, CH), F32),
            jax.ShapeDtypeStruct((1, 2, CH), F32),
        ),
        in_specs=[vmem, vmem, vmem, vmem, anywhere, anywhere],
        out_specs=(vmem, vmem, vmem),
        scratch_shapes=[
            pltpu.VMEM((8, WEIGHT_ROWS, CH), BF16),
            pltpu.VMEM((8, 8, CH), F32),
            pltpu.VMEM((9, CELLS, CH), BF16),
            pltpu.VMEM((9, CELLS, CH), BF16),
            pltpu.VMEM((8, CELLS, CH), F32),
            pltpu.VMEM((8, CELLS, CH), F32),
            pltpu.VMEM((8, 8, CH), F32),
            pltpu.VMEM((CELLS, SPATIAL), BF16),
            pltpu.VMEM((CELLS, 3 * CH), BF16),
            pltpu.VMEM((CH, CELLS), BF16),
            pltpu.VMEM((CH, CELLS), BF16),
            pltpu.VMEM((4, 4, 192, CH), BF16),
            pltpu.VMEM((2, 4, 4, 192, HALF), BF16),
            pltpu.VMEM((2, 4, 192, HALF), BF16),
            pltpu.VMEM((2, 4, 192, HALF), BF16),
            pltpu.VMEM((4, 48, CH), F32),
            pltpu.VMEM((4, 48, CH), BF16),
            pltpu.VMEM((4, 48, CH), BF16),
            pltpu.VMEM((3, 4, 8, CH), F32),
            dma((2,)),
            dma((4, 2)), dma((3, 2)),
            dma((3, 2, 4)), dma((3, 2, 4)),
            dma((3, 2, 4)), dma((3, 2, 4)),
            dma((4,)), dma((4,)),
            dma((8,)), dma((8,)),
            dma((2, 4)), dma((2, 4)),
            dma((2, 4)), dma((2, 4)),
            dma((4,)), dma((4,)),
            dma((3, 4)), dma((3, 4)),
        ],
        compiler_params=pltpu.CompilerParams(
            collective_id=0, has_side_effects=True, vmem_limit_bytes=56 * 1024 * 1024
        ),
        cost_estimate=pl.CostEstimate(
            flops=2 * 256 * 256 * 3072 * 17, bytes_accessed=4 * 1024 * 1024, transcendentals=8 * 65536
        ),
    )(
        latents.reshape(CELLS, CH), cotangent.reshape(CELLS, CH), norm_gain, norm_shift,
        spatial_weight, temporal_weight,
    )


def solution(mesh):
    return jax.shard_map(
        shards,
        mesh=mesh,
        in_specs=(
            P("dp", None, None, None, None),
            P("dp", None, None, None, None),
            P("section", None, None),
            P("section", None, None),
            P("section", None),
            P("section", None),
        ),
        out_specs=(P("section", "dp", None), P("section", "dp", None), P("section", None, None)),
        check_vma=False,
    )
```

```python
import functools

import jax
import jax.numpy as jnp
from jax import lax
from jax.experimental import pallas as pl
from jax.experimental.pallas import tpu as pltpu
from jax.sharding import PartitionSpec as P

MESH = pl.DeviceIdType.MESH
EPSILON = 1e-05
CELLS = 256
CH = 256
HALF = 128
SPATIAL = 2304
WEIGHT_ROWS = 3072
SLICE = WEIGHT_ROWS // 16
LONG = WEIGHT_ROWS // 4
BIT = SLICE // 4
SPATIAL_OFFSETS = tuple((dy, dx) for dy in (-1, 0, 1) for dx in (-1, 0, 1))
TEMPORAL_OFFSETS = (-1, 0, 1)
F32 = jnp.float32
BF16 = jnp.bfloat16


def group_mean(value):
    lane = lax.broadcasted_iota(jnp.int32, value.shape, 1)
    for step in (1, 2, 4):
        after = pltpu.roll(value, CH - step, axis=1)
        before = pltpu.roll(value, step, axis=1)
        value = value + jnp.where((lane & step) == 0, after, before)
    return value * 0.125


def over_groups(row_sum):
    wide = jnp.broadcast_to(row_sum * (1.0 / CELLS), (8, CH))
    return group_mean(wide)[0:1]


def shift_x(value, dx):
    if dx == 0:
        return value
    lines = value.reshape(32, 8, CH)
    moved = pltpu.roll(lines, (-dx) % 8, axis=1)
    column = lax.broadcasted_iota(jnp.int32, lines.shape, 1)
    inside = column != (7 if dx == 1 else 0)
    return jnp.where(inside, moved, 0.0).reshape(CELLS, CH)


def shift_y(value, dy):
    if dy == 0:
        return value
    frames = value.reshape(4, 64, CH)
    edge = jnp.zeros((4, 8, CH), value.dtype)
    if dy == 1:
        frames = jnp.concatenate([frames[:, 8:], edge], axis=1)
    else:
        frames = jnp.concatenate([edge, frames[:, :56]], axis=1)
    return frames.reshape(CELLS, CH)


def shift_t(value, dt):
    if dt == 0:
        return value
    edge = jnp.zeros((64, CH), value.dtype)
    if dt == 1:
        return jnp.concatenate([value[64:], edge], axis=0)
    return jnp.concatenate([edge, value[:192]], axis=0)


def fill_spatial(cols, value, sign):
    for dx in (-1, 0, 1):
        moved = shift_x(value, sign * dx)
        for dy in (-1, 0, 1):
            tap = SPATIAL_OFFSETS.index((dy, dx))
            cols[:, tap * CH : (tap + 1) * CH] = shift_y(moved, sign * dy).astype(BF16)


def fill_temporal(cols, value, sign):
    for tap, dt in enumerate(TEMPORAL_OFFSETS):
        cols[:, tap * CH : (tap + 1) * CH] = shift_t(value, sign * dt)


def times_transposed(left, right):
    return lax.dot_general(left, right, (((1,), (1,)), ((), ())), preferred_element_type=F32)


def kernel(
    latents, cotangent, gain_ref, shift_ref, spatial_ref, temporal_ref,
    packed_out,
    wall, prm, hist, ghist, normed_s, slope_s, scale_s, cols, tcols, act_t, mid_t,
    gsend, first_in, first_sum, second_in, third_f, third_out, third_in, norm_acc,
    local_sem, own_send, own_recv, z_send, z_recv, relay_send, line_send, line_recv,
    mid_send, mid_recv, last_send, last_recv, far_send, far_recv, core_send, core_recv,
    prm_send, prm_recv, prm_core_send, prm_core_recv,
    g1_send, g1_recv, g2_send, g2_recv, g3_send, g3_recv, n_send, n_recv,
):
    dp = lax.axis_index("dp")
    pos = lax.axis_index("section")
    px = dp // 16
    py = (dp // 4) % 4
    pz = dp % 4
    block = pos // 2
    core = pos % 2

    def at_x(x):
        return (x * 16 + py * 4 + pz, pos)

    def at_y(y):
        return (px * 16 + y * 4 + pz, pos)

    def at_z(z):
        return (px * 16 + py * 4 + z, pos)

    def at_section(s):
        return (dp, s)

    def copy(src, dst, send, recv, device):
        return pltpu.make_async_remote_copy(
            src_ref=src, dst_ref=dst, send_sem=send, recv_sem=recv,
            device_id=device, device_id_type=MESH,
        )

    along = ((px, at_x), (py, at_y))

    loads = [
        pltpu.make_async_copy(spatial_ref.at[0], wall.at[pos, pl.ds(0, SPATIAL)], local_sem.at[0]),
        pltpu.make_async_copy(
            temporal_ref.at[0], wall.at[pos, pl.ds(SPATIAL, WEIGHT_ROWS - SPATIAL)], local_sem.at[1]
        ),
    ]
    for load in loads:
        load.start()

    barrier = pltpu.get_barrier_semaphore()
    for d in (1, 2, 3):
        for mine, place in along + ((pz, at_z),):
            pl.semaphore_signal(
                barrier, inc=1, device_id=place((mine + d) % 4), device_id_type=MESH
            )
    for other in (pos + 2, pos + 6, pos + 1 - 2 * core):
        pl.semaphore_signal(
            barrier, inc=1, device_id=at_section(other % 8), device_id_type=MESH
        )

    rest = jnp.zeros((6, CH), F32)
    prm[pos] = jnp.concatenate([gain_ref[...], shift_ref[...], rest], axis=0)
    hist[0] = latents[...]
    ghist[8] = cotangent[...]
    for load in loads:
        load.wait()
    pl.semaphore_wait(barrier, 12)

    other_core = at_section(pos + 1 - 2 * core)
    after = (block + 1) % 4
    behind = (block + 3) % 4

    def order(pair, seen_from):
        return jnp.where(pair < seen_from, pair, pair - 1)

    def pair_of(k):
        return jnp.where(k < block, k, k + 1)

    def section_of(k):
        return 2 * pair_of(k) + core

    def part(section, row, rows, half):
        return wall.at[section, pl.ds(row, rows), pl.ds(half * HALF, HALF)]

    def slice_row(m, n):
        return (n * 4 + m) * SLICE

    def own_copy():
        return copy(wall.at[pos], wall.at[pos], own_send.at[0], own_recv.at[0], other_core)

    def own_arrival():
        ref = wall.at[pos + 1 - 2 * core]
        return copy(ref, ref, own_send.at[0], own_recv.at[0], other_core)

    def bit(section, half, line):
        m, n = along[half][0], along[1 - half][0]
        return part(section, slice_row(m, n) + line * BIT, BIT, half)

    targets = (after, behind)

    def z_copy(way, half):
        target = targets[way]
        ref = bit(pos, half, pz)
        return copy(
            ref, ref, z_send.at[way, half], z_recv.at[order(block, target), half],
            at_section(target * 2 + core),
        )

    def z_arrival(k, half):
        ref = bit(section_of(k), half, pz)
        return copy(ref, ref, z_send.at[0, half], z_recv.at[k, half], at_section(after * 2 + core))

    def relay_copy(way):
        pair, target = (behind, after) if way == 0 else (after, behind)
        ref = bit(2 * pair + core, way, pz)
        return copy(
            ref, ref, relay_send.at[way], z_recv.at[order(pair, target), way],
            at_section(target * 2 + core),
        )

    def prm_copy(way):
        section = 2 * behind + core if way == 2 else pos
        target = after if way == 2 else targets[way]
        pair = behind if way == 2 else block
        return copy(
            prm.at[section], prm.at[section], prm_send.at[way], prm_recv.at[order(pair, target)],
            at_section(target * 2 + core),
        )

    def prm_arrival(k):
        ref = prm.at[section_of(k)]
        return copy(ref, ref, prm_send.at[0], prm_recv.at[k], at_section(after * 2 + core))

    def prm_core_copy(pair):
        ref = prm.at[2 * pair + core]
        return copy(ref, ref, prm_core_send.at[pair], prm_core_recv.at[pair], other_core)

    def prm_core_arrival(pair):
        ref = prm.at[2 * pair + 1 - core]
        return copy(ref, ref, prm_core_send.at[pair], prm_core_recv.at[pair], other_core)

    def line_copy(k, half, d):
        ref = bit(section_of(k), half, pz)
        return copy(
            ref, ref, line_send.at[k, half, d], line_recv.at[k, half, pz], at_z((pz + d) % 4)
        )

    def line_arrival(k, half, d):
        source = (pz + d) % 4
        ref = bit(section_of(k), half, source)
        return copy(ref, ref, line_send.at[k, half, d], line_recv.at[k, half, source], at_z(source))

    def mid_copy(k, half, slot, arrival=False):
        (m, place), n = along[half], along[1 - half][0]
        step = 1 if slot % 2 == 0 else 3
        if arrival:
            step = 4 - step
        target = place((m + step) % 4)
        if slot < 2:
            source = (m + step) % 4 if arrival else m
            row, rows = slice_row(source, n), SLICE
        else:
            source = (m + 2) % 4 if arrival else (m + 4 - step) % 4
            row, rows = slice_row(source, n) + (slot - 2) * (SLICE // 2), SLICE // 2
        ref = part(section_of(k), row, rows, half)
        return copy(ref, ref, mid_send.at[k, half, slot], mid_recv.at[k, half, slot], target)

    def last_copy(k, half, way, index, arrival=False):
        m, (n, place) = along[half][0], along[1 - half]
        step = 1 if way == 0 else 3
        if arrival:
            step = 4 - step
        slab = (n + step) % 4 if arrival else n
        row = slice_row((m + (0, 3, 1, 2)[index]) % 4, slab)
        ref = part(section_of(k), row, SLICE, half)
        return copy(
            ref, ref, last_send.at[k, half, way, index], last_recv.at[k, half, way, index],
            place((n + step) % 4),
        )

    def far_copy(k, half, index, arrival=False):
        m, (n, place) = along[half][0], along[1 - half]
        step = 1 if index < 2 else 3
        if arrival:
            step = 4 - step
        slab = (n + 2) % 4 if arrival else (n + 4 - step) % 4
        row = slice_row((m + (0, 3, 1, 2)[index]) % 4, slab)
        ref = part(section_of(k), row, SLICE, half)
        return copy(
            ref, ref, far_send.at[k, half, index], far_recv.at[k, half, index],
            place((n + step) % 4),
        )

    def core_copy(k, half, index, arrival=False):
        n = along[1 - half][0]
        section = 2 * pair_of(k) + (1 - core if arrival else core)
        ref = part(section, ((n + (0, 3, 1, 2)[index]) % 4) * LONG, LONG, half)
        return copy(
            ref, ref, core_send.at[k, half, index], core_recv.at[k, half, index], other_core
        )

    def act_a(pair, relay):
        k = order(pair, block)
        for half in (0, 1):
            z_arrival(k, half).wait_recv()
            if relay == half:
                relay_copy(half).start()
            for d in (1, 3, 2):
                line_copy(k, half, d).start()
        prm_arrival(k).wait_recv()
        if relay == 0:
            prm_copy(2).start()
        prm_core_copy(pair).start()

    def act_b(k):
        for half in (0, 1):
            for d in (1, 3, 2):
                line_arrival(k, half, d).wait_recv()
            for slot in (0, 1):
                mid_copy(k, half, slot).start()
            for way in (0, 1):
                last_copy(k, half, way, 0).start()

    def act_c(k):
        for half in (0, 1):
            for slot in (0, 1):
                mid_copy(k, half, slot, True).wait_recv()
            for slot in (2, 3):
                mid_copy(k, half, slot).start()
            for index in (1, 2):
                for way in (0, 1):
                    last_copy(k, half, way, index).start()

    def act_d(k):
        for half in (0, 1):
            for slot in (2, 3):
                mid_copy(k, half, slot, True).wait_recv()
            for way in (0, 1):
                last_copy(k, half, way, 3).start()
            core_copy(k, half, 0).start()

    def act_e(k):
        for half in (0, 1):
            for index in (0, 1):
                last_copy(k, half, 0, index, True).wait_recv()
                far_copy(k, half, index).start()
            for index in (2, 3):
                last_copy(k, half, 1, index, True).wait_recv()
                far_copy(k, half, index).start()

    def act_f(k):
        for half in (0, 1):
            for index in (2, 3):
                last_copy(k, half, 0, index, True).wait_recv()
            core_copy(k, half, 1).start()
            for index in (0, 1):
                last_copy(k, half, 1, index, True).wait_recv()
            core_copy(k, half, 2).start()

    def act_g(k):
        for half in (0, 1):
            for index in range(4):
                far_copy(k, half, index, True).wait_recv()
            core_copy(k, half, 3).start()

    def act_h(k):
        for half in (0, 1):
            for index in range(4):
                core_copy(k, half, index, True).wait_recv()
        prm_core_arrival(pair_of(k)).wait_recv()

    for half in (0, 1):
        for way in (0, 1):
            z_copy(way, half).start()
    for way in (0, 1):
        prm_copy(way).start()
    prm_core_copy(block).start()
    own_copy().start()

    def gather_start():
        act_a(behind, 0)
        act_a(after, 1)
        far_first = block == 2
        pl.when(jnp.logical_not(far_first))(lambda: act_b(0))
        act_a((block + 2) % 4, None)
        pl.when(far_first)(lambda: act_b(0))
        act_b(1)
        act_c(0)
        act_d(0)
        act_c(1)
        act_e(0)
        act_b(2)
        act_d(1)
        act_f(0)
        act_c(2)
        act_g(0)
        act_e(1)
        act_d(2)

    def gather_sent():
        def one(k, carry):
            for half in (0, 1):
                for d in (1, 3, 2):
                    line_copy(k, half, d).wait_send()
                for index in range(4):
                    mid_copy(k, half, index).wait_send()
                    for way in (0, 1):
                        last_copy(k, half, way, index).wait_send()
                    far_copy(k, half, index).wait_send()
                    core_copy(k, half, index).wait_send()
            return carry

        for half in (0, 1):
            for way in (0, 1):
                z_copy(way, half).wait_send()
            relay_copy(half).wait_send()
        for way in range(3):
            prm_copy(way).wait_send()
        for pair in range(4):
            prm_core_copy(pair).wait_send()
        own_copy().wait_send()
        lax.fori_loop(0, 3, one, 0)

    def forward(s):
        params = prm[s]
        gain = params[0:1]
        shift = params[1:2]
        decoder = s >= 4
        skip = jnp.where(decoder, 1.0, 0.0)
        inputs = hist[s].astype(F32) + skip * hist[jnp.where(decoder, 8 - s, 0)].astype(F32)
        center = over_groups(jnp.sum(inputs, axis=0, keepdims=True))
        deviation = inputs - center
        variance = over_groups(jnp.sum(deviation * deviation, axis=0, keepdims=True))
        scaling = lax.rsqrt(variance + EPSILON)
        normed = deviation * scaling
        before = normed * gain + shift
        sigma = jax.nn.sigmoid(before)
        normed_s[s] = normed
        slope_s[s] = sigma * (1.0 + before * (1.0 - sigma))
        scale_s[s] = jnp.broadcast_to(scaling, (8, CH))

        @pl.when((s < 7) | (pos == 7))
        def _():
            active = before * sigma
            fill_spatial(cols, active, 1)
            middle = jnp.dot(cols[...], wall[s, 0:SPATIAL], preferred_element_type=F32)
            rounded = middle.astype(BF16)
            fill_temporal(tcols, rounded, 1)
            branch = jnp.dot(tcols[...], wall[s, SPATIAL:WEIGHT_ROWS], preferred_element_type=F32)
            hist[s + 1] = (inputs + branch).astype(BF16)

            @pl.when(s == pos)
            def _():
                act_t[...] = active.T.astype(BF16)
                mid_t[...] = middle.T.astype(BF16)

    def forward_pair(pair, carry):
        foreign = pair != block
        k = order(pair, block)

        @pl.when(pair == jnp.where(block == 0, 1, 0))
        def _():
            gather_start()

        @pl.when(foreign)
        def _():
            act_h(k)

        @pl.when(pair == block)
        def _():
            own_arrival().wait_recv()
            prm_core_arrival(block).wait_recv()

        def one(index, inner):
            forward(2 * pair + index)

            @pl.when(foreign & (k < 2) & (index == 0))
            def _():
                act_f(k + 1)

            @pl.when(foreign & (k < 2) & (index == 1))
            def _():
                act_g(k + 1)

            @pl.when(foreign & (k < 1) & (index == 1))
            def _():
                act_e(k + 2)

            return inner

        return lax.fori_loop(0, 2, one, carry)

    lax.fori_loop(0, 4, forward_pair, 0)

    def upstream(s):
        encoder = s < 4
        extra = jnp.where(encoder, 1.0, 0.0)
        other = ghist[jnp.where(encoder, 7 - s, 8)].astype(F32)
        return (ghist[s + 1].astype(F32) + extra * other).astype(BF16)

    def middle_grad(s, up):
        fill_temporal(tcols, up, -1)
        total = jnp.zeros((CELLS, CH), F32)
        for tap in range(3):
            weight = wall[s, SPATIAL + tap * CH : SPATIAL + (tap + 1) * CH]
            total = total + times_transposed(tcols[:, tap * CH : (tap + 1) * CH], weight)
        fill_spatial(cols, total, -1)

    def before_grad(s):
        total = jnp.zeros((CELLS, CH), F32)
        for tap in range(9):
            weight = wall[s, tap * CH : (tap + 1) * CH]
            total = total + times_transposed(cols[:, tap * CH : (tap + 1) * CH], weight)
        return total * slope_s[s]

    def backward(i, carry):
        s = 7 - i
        gain = prm[s][0:1]
        up = upstream(s)
        middle_grad(s, up)
        grad = before_grad(s)
        normed = normed_s[s]
        inner = over_groups(gain * jnp.sum(grad, axis=0, keepdims=True))
        project = over_groups(gain * jnp.sum(grad * normed, axis=0, keepdims=True))
        input_grad = scale_s[s][0:1] * (grad * gain - inner - normed * project)
        ghist[s] = (up.astype(F32) + input_grad).astype(BF16)
        return carry

    lax.fori_loop(0, 7 - pos, backward, 0)

    def store_rows(tile, row, per_x, per_y, base):
        end = row + CH
        while row < end:
            stop = min(end, (row // per_y + 1) * per_y)
            where_x = row // per_x
            where_y = (row % per_x) // per_y
            inside = row % per_y
            start = CH - (end - row)
            gsend[where_x, where_y, base + inside : base + inside + stop - row, :] = tile[
                start : start + stop - row
            ]
            row = stop

    up = upstream(pos)
    middle_grad(pos, up)
    for tap in range(3):
        tile = jnp.dot(mid_t[...], tcols[:, tap * CH : (tap + 1) * CH], preferred_element_type=F32)
        store_rows(tile.astype(BF16), tap * CH, 192, 48, 144)
    for tap in range(9):
        tile = jnp.dot(act_t[...], cols[:, tap * CH : (tap + 1) * CH], preferred_element_type=F32)
        store_rows(tile.astype(BF16), tap * CH, 576, 144, 0)

    def own_part(half, index):
        if half == 0:
            return gsend.at[index, :, :, pl.ds(0, HALF)]
        return gsend.at[:, index, :, pl.ds(HALF, HALF)]

    def g1_copy(half, d):
        mine, place = along[half]
        target = (mine + d) % 4
        return copy(
            own_part(half, target), first_in.at[half, mine], g1_send.at[half, d],
            g1_recv.at[half, mine], place(target),
        )

    def g1_arrival(half, d):
        mine, place = along[half]
        source = (mine + d) % 4
        return copy(
            own_part(half, source), first_in.at[half, source], g1_send.at[half, d],
            g1_recv.at[half, source], place(source),
        )

    def g2_copy(half, d):
        mine, place = along[1 - half]
        target = (mine + d) % 4
        return copy(
            first_sum.at[half, target], second_in.at[half, mine], g2_send.at[half, d],
            g2_recv.at[half, mine], place(target),
        )

    def g2_arrival(half, d):
        mine, place = along[1 - half]
        source = (mine + d) % 4
        return copy(
            first_sum.at[half, source], second_in.at[half, source], g2_send.at[half, d],
            g2_recv.at[half, source], place(source),
        )

    def g3_copy(d):
        target = (pz + d) % 4
        return copy(
            third_out.at[target], third_in.at[pz], g3_send.at[d], g3_recv.at[pz], at_z(target)
        )

    def g3_arrival(d):
        source = (pz + d) % 4
        return copy(
            third_out.at[source], third_in.at[source], g3_send.at[d], g3_recv.at[source], at_z(source)
        )

    for half in (0, 1):
        for d in (1, 3, 2):
            g1_copy(half, d).start()

    axes = along + ((pz, at_z),)

    def n_copy(phase, d):
        mine, place = axes[phase]
        return copy(
            norm_acc.at[phase, mine], norm_acc.at[phase, mine], n_send.at[phase, d],
            n_recv.at[phase, mine], place((mine + d) % 4),
        )

    def n_arrival(phase, d):
        mine, place = axes[phase]
        source = (mine + d) % 4
        return copy(
            norm_acc.at[phase, source], norm_acc.at[phase, source], n_send.at[phase, d],
            n_recv.at[phase, source], place(source),
        )

    grad = before_grad(pos)
    gain_term = jnp.sum(grad * normed_s[pos], axis=0, keepdims=True)
    shift_term = jnp.sum(grad, axis=0, keepdims=True)
    norm_value = jnp.concatenate([gain_term, shift_term, rest], axis=0)

    def norm_start(phase, value):
        norm_acc[phase, axes[phase][0]] = value
        for d in (1, 3, 2):
            n_copy(phase, d).start()

    def norm_finish(phase):
        for d in (1, 3, 2):
            n_arrival(phase, d).wait_recv()
        return ((norm_acc[phase, 0] + norm_acc[phase, 1]) + norm_acc[phase, 2]) + norm_acc[phase, 3]

    norm_start(0, norm_value)
    gather_sent()

    for half in (0, 1):
        mine = along[half][0]
        for d in (1, 3, 2):
            g1_arrival(half, d).wait_recv()
        for index in range(4):
            if half == 0:
                total = gsend[mine, index, :, 0:HALF].astype(F32)
            else:
                total = gsend[index, mine, :, HALF:CH].astype(F32)
            for d in (1, 2, 3):
                total = total + first_in[half, (mine + d) % 4, index].astype(F32)
            first_sum[half, index] = total.astype(BF16)
        for d in (1, 3, 2):
            g2_copy(half, d).start()

    norm_start(1, norm_finish(0))

    for half in (0, 1):
        mine = along[1 - half][0]
        for d in (1, 3, 2):
            g2_arrival(half, d).wait_recv()
        total = first_sum[half, mine].astype(F32)
        for d in (1, 2, 3):
            total = total + second_in[half, (mine + d) % 4].astype(F32)
        columns = slice(half * HALF, (half + 1) * HALF)
        for z in range(4):
            third_f[z, 0:36, columns] = total[z * 36 : (z + 1) * 36]
            third_f[z, 36:48, columns] = total[144 + z * 12 : 144 + (z + 1) * 12]
    for z in range(4):
        third_out[z] = third_f[z].astype(BF16)
    for d in (1, 3, 2):
        g3_copy(d).start()

    norm_start(2, norm_finish(1))

    total = third_f[pz]
    for d in (1, 3, 2):
        g3_arrival(d).wait_recv()
    for d in (1, 2, 3):
        total = total + third_in[(pz + d) % 4].astype(F32)
    packed_out[0:48] = total
    packed_out[48:56] = norm_finish(2)

    for d in (1, 3, 2):
        for half in (0, 1):
            g1_copy(half, d).wait_send()
            g2_copy(half, d).wait_send()
        g3_copy(d).wait_send()
        for phase in range(3):
            n_copy(phase, d).wait_send()


def unpack(packed, spatial_out, temporal_out, norm_out):
    spatial_out[...] = packed[0:36].reshape(36, 1, CH)
    temporal_out[...] = packed[36:48].reshape(12, 1, CH)
    norm_out[0] = packed[48:50]


def shards(latents, cotangent, spatial_weight, temporal_weight, norm_gain, norm_shift):
    vmem = pl.BlockSpec(memory_space=pltpu.VMEM)
    anywhere = pl.BlockSpec(memory_space=pl.ANY)
    dma = pltpu.SemaphoreType.DMA
    packed = pl.pallas_call(
        kernel,
        out_shape=jax.ShapeDtypeStruct((56, CH), F32),
        in_specs=[vmem, vmem, vmem, vmem, anywhere, anywhere],
        out_specs=vmem,
        scratch_shapes=[
            pltpu.VMEM((8, WEIGHT_ROWS, CH), BF16),
            pltpu.VMEM((8, 8, CH), F32),
            pltpu.VMEM((9, CELLS, CH), BF16),
            pltpu.VMEM((9, CELLS, CH), BF16),
            pltpu.VMEM((8, CELLS, CH), F32),
            pltpu.VMEM((8, CELLS, CH), F32),
            pltpu.VMEM((8, 8, CH), F32),
            pltpu.VMEM((CELLS, SPATIAL), BF16),
            pltpu.VMEM((CELLS, 3 * CH), BF16),
            pltpu.VMEM((CH, CELLS), BF16),
            pltpu.VMEM((CH, CELLS), BF16),
            pltpu.VMEM((4, 4, 192, CH), BF16),
            pltpu.VMEM((2, 4, 4, 192, HALF), BF16),
            pltpu.VMEM((2, 4, 192, HALF), BF16),
            pltpu.VMEM((2, 4, 192, HALF), BF16),
            pltpu.VMEM((4, 48, CH), F32),
            pltpu.VMEM((4, 48, CH), BF16),
            pltpu.VMEM((4, 48, CH), BF16),
            pltpu.VMEM((3, 4, 8, CH), F32),
            dma((2,)),
            dma((1,)), dma((1,)),
            dma((2, 2)), dma((3, 2)), dma((2,)),
            dma((3, 2, 4)), dma((3, 2, 4)),
            dma((3, 2, 4)), dma((3, 2, 4)),
            dma((3, 2, 2, 4)), dma((3, 2, 2, 4)),
            dma((3, 2, 4)), dma((3, 2, 4)),
            dma((3, 2, 4)), dma((3, 2, 4)),
            dma((3,)), dma((3,)),
            dma((4,)), dma((4,)),
            dma((2, 4)), dma((2, 4)),
            dma((2, 4)), dma((2, 4)),
            dma((4,)), dma((4,)),
            dma((3, 4)), dma((3, 4)),
        ],
        compiler_params=pltpu.CompilerParams(
            collective_id=0, has_side_effects=True, vmem_limit_bytes=56 * 1024 * 1024
        ),
        cost_estimate=pl.CostEstimate(
            flops=2 * 256 * 256 * 3072 * 17, bytes_accessed=4 * 1024 * 1024, transcendentals=8 * 65536
        ),
    )(
        latents.reshape(CELLS, CH), cotangent.reshape(CELLS, CH), norm_gain, norm_shift,
        spatial_weight, temporal_weight,
    )
    spatial, temporal, norm = pl.pallas_call(
        unpack,
        out_shape=(
            jax.ShapeDtypeStruct((36, 1, CH), F32),
            jax.ShapeDtypeStruct((12, 1, CH), F32),
            jax.ShapeDtypeStruct((1, 2, CH), F32),
        ),
        in_specs=[vmem],
        out_specs=(vmem, vmem, vmem),
    )(packed)
    return (spatial.transpose(1, 0, 2), temporal.transpose(1, 0, 2), norm)


def solution(mesh):
    return jax.shard_map(
        shards,
        mesh=mesh,
        in_specs=(
            P("dp", None, None, None, None),
            P("dp", None, None, None, None),
            P("section", None, None),
            P("section", None, None),
            P("section", None),
            P("section", None),
        ),
        out_specs=(P("section", "dp", None), P("section", "dp", None), P("section", None, None)),
        check_vma=False,
    )
```

```python
import functools

import jax
import jax.numpy as jnp
from jax import lax
from jax.experimental import pallas as pl
from jax.experimental.pallas import tpu as pltpu
from jax.sharding import PartitionSpec as P

MESH = pl.DeviceIdType.MESH
EPSILON = 1e-05
CELLS = 256
CH = 256
HALF = 128
SPATIAL = 2304
WEIGHT_ROWS = 3072
SLICE = WEIGHT_ROWS // 16
LONG = WEIGHT_ROWS // 4
BIT = SLICE // 4
SUB = SLICE // 2
SPATIAL_OFFSETS = tuple((dy, dx) for dy in (-1, 0, 1) for dx in (-1, 0, 1))
TEMPORAL_OFFSETS = (-1, 0, 1)
F32 = jnp.float32
BF16 = jnp.bfloat16


def group_values(first, second):
    rest = jnp.zeros((4, HALF), F32)
    rows = [first[:, :HALF], first[:, HALF:], second[:, :HALF], second[:, HALF:], rest]
    value = jnp.concatenate(rows, axis=0)
    place = lax.broadcasted_iota(jnp.int32, value.shape, 1) % 8
    values = [value]
    for step in range(1, 8):
        ahead = pltpu.roll(value, HALF - step, axis=1)
        back = pltpu.roll(value, 8 - step, axis=1)
        values.append(jnp.where(place < 8 - step, ahead, back))
    return values


def added(values):
    while len(values) > 1:
        values = [a + b for a, b in zip(values[::2], values[1::2])]
    return values[0]


def widened(rows):
    return jnp.concatenate([rows[0:1], rows[1:2]], axis=1)


def group_statistics(inputs):
    column = jnp.sum(inputs, axis=0, keepdims=True) * (1.0 / CELLS)
    within = inputs - column
    spread = jnp.sum(within * within, axis=0, keepdims=True) * (1.0 / CELLS)
    values = group_values(column, spread)
    mean = added(values) * 0.125
    between = added([(value - mean) * (value - mean) for value in values]) * 0.125
    scaling = lax.rsqrt(mean[2:4] + between[0:2] + EPSILON)
    return widened(mean[0:2]), widened(scaling)


def group_means(first, second):
    mean = added(group_values(first, second)) * (0.125 / CELLS)
    return widened(mean[0:2]), widened(mean[2:4])


def shift_x(value, dx):
    if dx == 0:
        return value
    lines = value.reshape(32, 8, CH)
    moved = pltpu.roll(lines, (-dx) % 8, axis=1)
    column = lax.broadcasted_iota(jnp.int32, lines.shape, 1)
    inside = column != (7 if dx == 1 else 0)
    return jnp.where(inside, moved, 0.0).reshape(CELLS, CH)


def shift_y(value, dy):
    if dy == 0:
        return value
    frames = value.reshape(4, 64, CH)
    edge = jnp.zeros((4, 8, CH), value.dtype)
    if dy == 1:
        frames = jnp.concatenate([frames[:, 8:], edge], axis=1)
    else:
        frames = jnp.concatenate([edge, frames[:, :56]], axis=1)
    return frames.reshape(CELLS, CH)


def shift_t(value, dt):
    if dt == 0:
        return value
    edge = jnp.zeros((64, CH), value.dtype)
    if dt == 1:
        return jnp.concatenate([value[64:], edge], axis=0)
    return jnp.concatenate([edge, value[:192]], axis=0)


def fill_spatial(cols, value, sign):
    for dx in (-1, 0, 1):
        moved = shift_x(value, sign * dx)
        for dy in (-1, 0, 1):
            tap = SPATIAL_OFFSETS.index((dy, dx))
            cols[:, tap * CH : (tap + 1) * CH] = shift_y(moved, sign * dy).astype(BF16)


def fill_temporal(cols, value, sign):
    for tap, dt in enumerate(TEMPORAL_OFFSETS):
        cols[:, tap * CH : (tap + 1) * CH] = shift_t(value, sign * dt)


def times_transposed(left, right):
    return lax.dot_general(left, right, (((1,), (1,)), ((), ())), preferred_element_type=F32)


def kernel(
    latents, cotangent, gain_ref, shift_ref, spatial_ref, temporal_ref,
    packed_out,
    wall, prm, hist, ghist, normed_s, slope_s, scale_s, cols, tcols, act_t, mid_t,
    gsend, first_in, first_sum, second_in, third_f, third_out, third_in, norm_acc,
    local_sem, own_send, own_recv, z_send, z_recv, relay_send, line_send, line_recv,
    mid_send, mid_recv, last_send, last_recv, far_send, far_recv, core_send, core_recv,
    prm_send, prm_recv, prm_core_send, prm_core_recv,
    g1_send, g1_recv, g2_send, g2_recv, g3_send, g3_recv, n_send, n_recv,
):
    dp = lax.axis_index("dp")
    pos = lax.axis_index("section")
    px = dp // 16
    py = (dp // 4) % 4
    pz = dp % 4
    block = pos // 2
    core = pos % 2

    def at_x(x):
        return (x * 16 + py * 4 + pz, pos)

    def at_y(y):
        return (px * 16 + y * 4 + pz, pos)

    def at_z(z):
        return (px * 16 + py * 4 + z, pos)

    def at_section(s):
        return (dp, s)

    def copy(src, dst, send, recv, device):
        return pltpu.make_async_remote_copy(
            src_ref=src, dst_ref=dst, send_sem=send, recv_sem=recv,
            device_id=device, device_id_type=MESH,
        )

    along = ((px, at_x), (py, at_y))

    loads = [
        pltpu.make_async_copy(spatial_ref.at[0], wall.at[pos, pl.ds(0, SPATIAL)], local_sem.at[0]),
        pltpu.make_async_copy(
            temporal_ref.at[0], wall.at[pos, pl.ds(SPATIAL, WEIGHT_ROWS - SPATIAL)], local_sem.at[1]
        ),
    ]
    for load in loads:
        load.start()

    barrier = pltpu.get_barrier_semaphore()
    for d in (1, 2, 3):
        for mine, place in along + ((pz, at_z),):
            pl.semaphore_signal(
                barrier, inc=1, device_id=place((mine + d) % 4), device_id_type=MESH
            )
    for other in (pos + 2, pos + 6, pos + 1 - 2 * core):
        pl.semaphore_signal(
            barrier, inc=1, device_id=at_section(other % 8), device_id_type=MESH
        )

    rest = jnp.zeros((6, CH), F32)
    prm[pos] = jnp.concatenate([gain_ref[...], shift_ref[...], rest], axis=0)
    hist[0] = latents[...]
    ghist[8] = cotangent[...]
    for load in loads:
        load.wait()
    pl.semaphore_wait(barrier, 12)

    other_core = at_section(pos + 1 - 2 * core)
    after = (block + 1) % 4
    behind = (block + 3) % 4

    def order(pair, seen_from):
        return jnp.where(pair < seen_from, pair, pair - 1)

    def pair_of(k):
        return jnp.where(k < block, k, k + 1)

    def section_of(k):
        return 2 * pair_of(k) + core

    def part(section, row, rows, half):
        return wall.at[section, pl.ds(row, rows), pl.ds(half * HALF, HALF)]

    def slice_row(m, n):
        return (n * 4 + m) * SLICE

    def own_copy():
        return copy(wall.at[pos], wall.at[pos], own_send.at[0], own_recv.at[0], other_core)

    def own_arrival():
        ref = wall.at[pos + 1 - 2 * core]
        return copy(ref, ref, own_send.at[0], own_recv.at[0], other_core)

    def bit(section, half, line):
        m, n = along[half][0], along[1 - half][0]
        return part(section, slice_row(m, n) + line * BIT, BIT, half)

    targets = (after, behind)

    def z_copy(way, half):
        target = targets[way]
        ref = bit(pos, half, pz)
        return copy(
            ref, ref, z_send.at[way, half], z_recv.at[order(block, target), half],
            at_section(target * 2 + core),
        )

    def z_arrival(k, half):
        ref = bit(section_of(k), half, pz)
        return copy(ref, ref, z_send.at[0, half], z_recv.at[k, half], at_section(after * 2 + core))

    def relay_copy(way):
        pair, target = (behind, after) if way == 0 else (after, behind)
        ref = bit(2 * pair + core, way, pz)
        return copy(
            ref, ref, relay_send.at[way], z_recv.at[order(pair, target), way],
            at_section(target * 2 + core),
        )

    def prm_copy(way):
        section = 2 * behind + core if way == 2 else pos
        target = after if way == 2 else targets[way]
        pair = behind if way == 2 else block
        return copy(
            prm.at[section], prm.at[section], prm_send.at[way], prm_recv.at[order(pair, target)],
            at_section(target * 2 + core),
        )

    def prm_arrival(k):
        ref = prm.at[section_of(k)]
        return copy(ref, ref, prm_send.at[0], prm_recv.at[k], at_section(after * 2 + core))

    def prm_core_copy(pair):
        ref = prm.at[2 * pair + core]
        return copy(ref, ref, prm_core_send.at[pair], prm_core_recv.at[pair], other_core)

    def prm_core_arrival(pair):
        ref = prm.at[2 * pair + 1 - core]
        return copy(ref, ref, prm_core_send.at[pair], prm_core_recv.at[pair], other_core)

    def line_copy(k, half, d):
        ref = bit(section_of(k), half, pz)
        return copy(
            ref, ref, line_send.at[k, half, d], line_recv.at[k, half, pz], at_z((pz + d) % 4)
        )

    def line_arrival(k, half, d):
        source = (pz + d) % 4
        ref = bit(section_of(k), half, source)
        return copy(ref, ref, line_send.at[k, half, d], line_recv.at[k, half, source], at_z(source))

    def mid_copy(k, half, slot, arrival=False):
        (m, place), n = along[half], along[1 - half][0]
        step = 1 if slot % 2 == 0 else 3
        if arrival:
            step = 4 - step
        target = place((m + step) % 4)
        if slot < 2:
            source = (m + step) % 4 if arrival else m
            row, rows = slice_row(source, n), SLICE
        else:
            source = (m + 2) % 4 if arrival else (m + 4 - step) % 4
            row, rows = slice_row(source, n) + (slot - 2) * (SLICE // 2), SLICE // 2
        ref = part(section_of(k), row, rows, half)
        return copy(ref, ref, mid_send.at[k, half, slot], mid_recv.at[k, half, slot], target)

    def last_copy(k, half, way, index, arrival=False):
        m, (n, place) = along[half][0], along[1 - half]
        step = 1 if way == 0 else 3
        if arrival:
            step = 4 - step
        slab = (n + step) % 4 if arrival else n
        row = slice_row((m + (0, 3, 1, 2)[index]) % 4, slab)
        ref = part(section_of(k), row, SLICE, half)
        return copy(
            ref, ref, last_send.at[k, half, way, index], last_recv.at[k, half, way, index],
            place((n + step) % 4),
        )

    def far_copy(k, half, index, arrival=False):
        m, (n, place) = along[half][0], along[1 - half]
        step = 1 if index < 2 else 3
        if arrival:
            step = 4 - step
        slab = (n + 2) % 4 if arrival else (n + 4 - step) % 4
        row = slice_row((m + (0, 3, 1, 2)[index]) % 4, slab)
        ref = part(section_of(k), row, SLICE, half)
        return copy(
            ref, ref, far_send.at[k, half, index], far_recv.at[k, half, index],
            place((n + step) % 4),
        )

    def core_copy(k, half, index, arrival=False):
        n = along[1 - half][0]
        section = 2 * pair_of(k) + (1 - core if arrival else core)
        ref = part(section, ((n + (0, 3, 1, 2)[index]) % 4) * LONG, LONG, half)
        return copy(
            ref, ref, core_send.at[k, half, index], core_recv.at[k, half, index], other_core
        )

    def act_a(pair, relay):
        k = order(pair, block)
        for half in (0, 1):
            z_arrival(k, half).wait_recv()
            if relay == half:
                relay_copy(half).start()
            for d in (1, 3, 2):
                line_copy(k, half, d).start()
        prm_arrival(k).wait_recv()
        if relay == 0:
            prm_copy(2).start()
        prm_core_copy(pair).start()

    def act_b(k):
        for half in (0, 1):
            for d in (1, 3, 2):
                line_arrival(k, half, d).wait_recv()
            for slot in (0, 1):
                mid_copy(k, half, slot).start()
            for way in (0, 1):
                last_copy(k, half, way, 0).start()

    def act_c(k):
        for half in (0, 1):
            for slot in (0, 1):
                mid_copy(k, half, slot, True).wait_recv()
            for slot in (2, 3):
                mid_copy(k, half, slot).start()
            for index in (1, 2):
                for way in (0, 1):
                    last_copy(k, half, way, index).start()

    def act_d(k):
        for half in (0, 1):
            for slot in (2, 3):
                mid_copy(k, half, slot, True).wait_recv()
            for way in (0, 1):
                last_copy(k, half, way, 3).start()
            core_copy(k, half, 0).start()

    def act_e(k):
        for half in (0, 1):
            for index in (0, 1):
                last_copy(k, half, 0, index, True).wait_recv()
                far_copy(k, half, index).start()
            for index in (2, 3):
                last_copy(k, half, 1, index, True).wait_recv()
                far_copy(k, half, index).start()

    def act_f(k):
        for half in (0, 1):
            for index in (2, 3):
                last_copy(k, half, 0, index, True).wait_recv()
            core_copy(k, half, 1).start()
            for index in (0, 1):
                last_copy(k, half, 1, index, True).wait_recv()
            core_copy(k, half, 2).start()

    def act_g(k):
        for half in (0, 1):
            for index in range(4):
                far_copy(k, half, index, True).wait_recv()
            core_copy(k, half, 3).start()

    def act_h(k):
        for half in (0, 1):
            for index in range(4):
                core_copy(k, half, index, True).wait_recv()
        prm_core_arrival(pair_of(k)).wait_recv()

    for half in (0, 1):
        for way in (0, 1):
            z_copy(way, half).start()
    for way in (0, 1):
        prm_copy(way).start()
    prm_core_copy(block).start()
    own_copy().start()

    def gather_start():
        act_a(behind, 0)
        act_a(after, 1)
        far_first = block == 2
        pl.when(jnp.logical_not(far_first))(lambda: act_b(0))
        act_a((block + 2) % 4, None)
        pl.when(far_first)(lambda: act_b(0))
        act_b(1)
        act_b(2)
        act_c(0)
        act_c(1)
        act_d(0)
        act_c(2)
        act_d(1)
        act_e(0)
        act_d(2)
        act_e(1)
        act_f(0)
        act_g(0)
        act_e(2)
        act_f(1)

    def gather_sent():
        def one(k, carry):
            for half in (0, 1):
                for d in (1, 3, 2):
                    line_copy(k, half, d).wait_send()
                for index in range(4):
                    mid_copy(k, half, index).wait_send()
                    for way in (0, 1):
                        last_copy(k, half, way, index).wait_send()
                    far_copy(k, half, index).wait_send()
                    core_copy(k, half, index).wait_send()
            return carry

        for half in (0, 1):
            for way in (0, 1):
                z_copy(way, half).wait_send()
            relay_copy(half).wait_send()
        for way in range(3):
            prm_copy(way).wait_send()
        for pair in range(4):
            prm_core_copy(pair).wait_send()
        own_copy().wait_send()
        lax.fori_loop(0, 3, one, 0)

    def forward(s):
        params = prm[s]
        gain = params[0:1]
        shift = params[1:2]
        decoder = s >= 4
        skip = jnp.where(decoder, 1.0, 0.0)
        inputs = hist[s].astype(F32) + skip * hist[jnp.where(decoder, 8 - s, 0)].astype(F32)
        center, scaling = group_statistics(inputs)
        normed = (inputs - center) * scaling
        before = normed * gain + shift
        sigma = jax.nn.sigmoid(before)
        normed_s[s] = normed
        slope_s[s] = sigma * (1.0 + before * (1.0 - sigma))
        scale_s[s] = jnp.broadcast_to(scaling, (8, CH))

        @pl.when((s < 7) | (pos == 7))
        def _():
            active = before * sigma
            fill_spatial(cols, active, 1)
            middle = jnp.dot(cols[...], wall[s, 0:SPATIAL], preferred_element_type=F32)
            rounded = middle.astype(BF16)
            fill_temporal(tcols, rounded, 1)
            branch = jnp.dot(tcols[...], wall[s, SPATIAL:WEIGHT_ROWS], preferred_element_type=F32)
            hist[s + 1] = (inputs + branch).astype(BF16)

            @pl.when(s == pos)
            def _():
                act_t[...] = active.T.astype(BF16)
                mid_t[...] = middle.T.astype(BF16)

    def forward_pair(pair, carry):
        foreign = pair != block
        k = order(pair, block)

        @pl.when(pair == jnp.where(block == 0, 1, 0))
        def _():
            gather_start()

        @pl.when(foreign)
        def _():
            act_h(k)

        @pl.when(pair == block)
        def _():
            own_arrival().wait_recv()
            prm_core_arrival(block).wait_recv()

        def one(index, inner):
            forward(2 * pair + index)

            @pl.when(foreign & (k == 0) & (index == 0))
            def _():
                act_g(1)
                act_f(2)

            @pl.when(foreign & (k == 0) & (index == 1))
            def _():
                act_g(2)

            return inner

        return lax.fori_loop(0, 2, one, carry)

    lax.fori_loop(0, 4, forward_pair, 0)

    def upstream(s):
        encoder = s < 4
        extra = jnp.where(encoder, 1.0, 0.0)
        other = ghist[jnp.where(encoder, 7 - s, 8)].astype(F32)
        return (ghist[s + 1].astype(F32) + extra * other).astype(BF16)

    def middle_grad(s, up):
        fill_temporal(tcols, up, -1)
        total = jnp.zeros((CELLS, CH), F32)
        for tap in range(3):
            weight = wall[s, SPATIAL + tap * CH : SPATIAL + (tap + 1) * CH]
            total = total + times_transposed(tcols[:, tap * CH : (tap + 1) * CH], weight)
        fill_spatial(cols, total, -1)

    def before_grad(s):
        total = jnp.zeros((CELLS, CH), F32)
        for tap in range(9):
            weight = wall[s, tap * CH : (tap + 1) * CH]
            total = total + times_transposed(cols[:, tap * CH : (tap + 1) * CH], weight)
        return total * slope_s[s]

    def backward(i, carry):
        s = 7 - i
        gain = prm[s][0:1]
        up = upstream(s)
        middle_grad(s, up)
        grad = before_grad(s)
        normed = normed_s[s]
        inner, project = group_means(
            gain * jnp.sum(grad, axis=0, keepdims=True),
            gain * jnp.sum(grad * normed, axis=0, keepdims=True),
        )
        input_grad = scale_s[s][0:1] * (grad * gain - inner - normed * project)
        ghist[s] = (up.astype(F32) + input_grad).astype(BF16)
        return carry

    lax.fori_loop(0, 7 - pos, backward, 0)

    def store_rows(tile, row, per_x, per_y, base):
        end = row + CH
        while row < end:
            stop = min(end, (row // per_y + 1) * per_y)
            where_x = row // per_x
            where_y = (row % per_x) // per_y
            inside = row % per_y
            start = CH - (end - row)
            gsend[where_x, where_y, base + inside : base + inside + stop - row, :] = tile[
                start : start + stop - row
            ]
            row = stop

    up = upstream(pos)
    middle_grad(pos, up)
    for tap in range(3):
        tile = jnp.dot(mid_t[...], tcols[:, tap * CH : (tap + 1) * CH], preferred_element_type=F32)
        store_rows(tile.astype(BF16), tap * CH, 192, 48, 144)
    for tap in range(9):
        tile = jnp.dot(act_t[...], cols[:, tap * CH : (tap + 1) * CH], preferred_element_type=F32)
        store_rows(tile.astype(BF16), tap * CH, 576, 144, 0)

    def own_part(half, index, sub):
        rows = pl.ds(sub * SUB, SUB)
        if half == 0:
            return gsend.at[index, :, rows, pl.ds(0, HALF)]
        return gsend.at[:, index, rows, pl.ds(HALF, HALF)]

    def g1_copy(half, sub, d, arrival=False):
        mine, place = along[half]
        other = (mine + d) % 4
        source = other if arrival else mine
        return copy(
            own_part(half, other, sub), first_in.at[half, source, :, pl.ds(sub * SUB, SUB)],
            g1_send.at[half, sub, d], g1_recv.at[half, sub, source], place(other),
        )

    def g2_copy(half, sub, d, arrival=False):
        mine, place = along[1 - half]
        other = (mine + d) % 4
        source = other if arrival else mine
        rows = pl.ds(sub * SUB, SUB)
        return copy(
            first_sum.at[half, other, rows], second_in.at[half, source, rows],
            g2_send.at[half, sub, d], g2_recv.at[half, sub, source], place(other),
        )

    def g3_copy(d):
        target = (pz + d) % 4
        return copy(
            third_out.at[target], third_in.at[pz], g3_send.at[d], g3_recv.at[pz], at_z(target)
        )

    def g3_arrival(d):
        source = (pz + d) % 4
        return copy(
            third_out.at[source], third_in.at[source], g3_send.at[d], g3_recv.at[source], at_z(source)
        )

    for sub in (0, 1):
        for half in (0, 1):
            for d in (1, 3, 2):
                g1_copy(half, sub, d).start()

    axes = along + ((pz, at_z),)

    def n_copy(phase, d):
        mine, place = axes[phase]
        return copy(
            norm_acc.at[phase, mine], norm_acc.at[phase, mine], n_send.at[phase, d],
            n_recv.at[phase, mine], place((mine + d) % 4),
        )

    def n_arrival(phase, d):
        mine, place = axes[phase]
        source = (mine + d) % 4
        return copy(
            norm_acc.at[phase, source], norm_acc.at[phase, source], n_send.at[phase, d],
            n_recv.at[phase, source], place(source),
        )

    grad = before_grad(pos)
    gain_term = jnp.sum(grad * normed_s[pos], axis=0, keepdims=True)
    shift_term = jnp.sum(grad, axis=0, keepdims=True)
    norm_value = jnp.concatenate([gain_term, shift_term, rest], axis=0)

    def norm_start(phase, value):
        norm_acc[phase, axes[phase][0]] = value
        for d in (1, 3, 2):
            n_copy(phase, d).start()

    def norm_finish(phase):
        for d in (1, 3, 2):
            n_arrival(phase, d).wait_recv()
        return ((norm_acc[phase, 0] + norm_acc[phase, 1]) + norm_acc[phase, 2]) + norm_acc[phase, 3]

    norm_start(0, norm_value)
    gather_sent()

    for sub in (0, 1):
        for half in (0, 1):
            mine = along[half][0]
            rows = slice(sub * SUB, (sub + 1) * SUB)
            for d in (1, 3, 2):
                g1_copy(half, sub, d, True).wait_recv()
            for index in range(4):
                if half == 0:
                    total = gsend[mine, index, rows, 0:HALF].astype(F32)
                else:
                    total = gsend[index, mine, rows, HALF:CH].astype(F32)
                for d in (1, 2, 3):
                    total = total + first_in[half, (mine + d) % 4, index, rows].astype(F32)
                first_sum[half, index, rows] = total.astype(BF16)
            for d in (1, 3, 2):
                g2_copy(half, sub, d).start()

    norm_start(1, norm_finish(0))

    for half in (0, 1):
        mine = along[1 - half][0]
        for sub in (0, 1):
            for d in (1, 3, 2):
                g2_copy(half, sub, d, True).wait_recv()
        total = first_sum[half, mine].astype(F32)
        for d in (1, 2, 3):
            total = total + second_in[half, (mine + d) % 4].astype(F32)
        columns = slice(half * HALF, (half + 1) * HALF)
        for z in range(4):
            third_f[z, 0:36, columns] = total[z * 36 : (z + 1) * 36]
            third_f[z, 36:48, columns] = total[144 + z * 12 : 144 + (z + 1) * 12]
    for z in range(4):
        third_out[z] = third_f[z].astype(BF16)
    for d in (1, 3, 2):
        g3_copy(d).start()

    norm_start(2, norm_finish(1))

    total = third_f[pz]
    for d in (1, 3, 2):
        g3_arrival(d).wait_recv()
    for d in (1, 2, 3):
        total = total + third_in[(pz + d) % 4].astype(F32)
    packed_out[0:48] = total
    packed_out[48:56] = norm_finish(2)

    for d in (1, 3, 2):
        for half in (0, 1):
            for sub in (0, 1):
                g1_copy(half, sub, d).wait_send()
                g2_copy(half, sub, d).wait_send()
        g3_copy(d).wait_send()
        for phase in range(3):
            n_copy(phase, d).wait_send()


def unpack(packed, spatial_out, temporal_out, norm_out):
    spatial_out[...] = packed[0:36].reshape(36, 1, CH)
    temporal_out[...] = packed[36:48].reshape(12, 1, CH)
    norm_out[0] = packed[48:50]


def shards(latents, cotangent, spatial_weight, temporal_weight, norm_gain, norm_shift):
    vmem = pl.BlockSpec(memory_space=pltpu.VMEM)
    anywhere = pl.BlockSpec(memory_space=pl.ANY)
    dma = pltpu.SemaphoreType.DMA
    packed = pl.pallas_call(
        kernel,
        out_shape=jax.ShapeDtypeStruct((56, CH), F32),
        in_specs=[vmem, vmem, vmem, vmem, anywhere, anywhere],
        out_specs=vmem,
        scratch_shapes=[
            pltpu.VMEM((8, WEIGHT_ROWS, CH), BF16),
            pltpu.VMEM((8, 8, CH), F32),
            pltpu.VMEM((9, CELLS, CH), BF16),
            pltpu.VMEM((9, CELLS, CH), BF16),
            pltpu.VMEM((8, CELLS, CH), F32),
            pltpu.VMEM((8, CELLS, CH), F32),
            pltpu.VMEM((8, 8, CH), F32),
            pltpu.VMEM((CELLS, SPATIAL), BF16),
            pltpu.VMEM((CELLS, 3 * CH), BF16),
            pltpu.VMEM((CH, CELLS), BF16),
            pltpu.VMEM((CH, CELLS), BF16),
            pltpu.VMEM((4, 4, 192, CH), BF16),
            pltpu.VMEM((2, 4, 4, 192, HALF), BF16),
            pltpu.VMEM((2, 4, 192, HALF), BF16),
            pltpu.VMEM((2, 4, 192, HALF), BF16),
            pltpu.VMEM((4, 48, CH), F32),
            pltpu.VMEM((4, 48, CH), BF16),
            pltpu.VMEM((4, 48, CH), BF16),
            pltpu.VMEM((3, 4, 8, CH), F32),
            dma((2,)),
            dma((1,)), dma((1,)),
            dma((2, 2)), dma((3, 2)), dma((2,)),
            dma((3, 2, 4)), dma((3, 2, 4)),
            dma((3, 2, 4)), dma((3, 2, 4)),
            dma((3, 2, 2, 4)), dma((3, 2, 2, 4)),
            dma((3, 2, 4)), dma((3, 2, 4)),
            dma((3, 2, 4)), dma((3, 2, 4)),
            dma((3,)), dma((3,)),
            dma((4,)), dma((4,)),
            dma((2, 2, 4)), dma((2, 2, 4)),
            dma((2, 2, 4)), dma((2, 2, 4)),
            dma((4,)), dma((4,)),
            dma((3, 4)), dma((3, 4)),
        ],
        compiler_params=pltpu.CompilerParams(
            collective_id=0, has_side_effects=True, vmem_limit_bytes=56 * 1024 * 1024
        ),
        cost_estimate=pl.CostEstimate(
            flops=2 * 256 * 256 * 3072 * 17, bytes_accessed=4 * 1024 * 1024, transcendentals=8 * 65536
        ),
    )(
        latents.reshape(CELLS, CH), cotangent.reshape(CELLS, CH), norm_gain, norm_shift,
        spatial_weight, temporal_weight,
    )
    spatial, temporal, norm = pl.pallas_call(
        unpack,
        out_shape=(
            jax.ShapeDtypeStruct((36, 1, CH), F32),
            jax.ShapeDtypeStruct((12, 1, CH), F32),
            jax.ShapeDtypeStruct((1, 2, CH), F32),
        ),
        in_specs=[vmem],
        out_specs=(vmem, vmem, vmem),
    )(packed)
    return (spatial.transpose(1, 0, 2), temporal.transpose(1, 0, 2), norm)


def solution(mesh):
    return jax.shard_map(
        shards,
        mesh=mesh,
        in_specs=(
            P("dp", None, None, None, None),
            P("dp", None, None, None, None),
            P("section", None, None),
            P("section", None, None),
            P("section", None),
            P("section", None),
        ),
        out_specs=(P("section", "dp", None), P("section", "dp", None), P("section", None, None)),
        check_vma=False,
    )
```

```python
import functools

import jax
import jax.numpy as jnp
from jax import lax
from jax.experimental import pallas as pl
from jax.experimental.pallas import tpu as pltpu
from jax.sharding import PartitionSpec as P

MESH = pl.DeviceIdType.MESH
EPSILON = 1e-05
CELLS = 256
CH = 256
HALF = 128
SPATIAL = 2304
WEIGHT_ROWS = 3072
SLICE = WEIGHT_ROWS // 16
LONG = WEIGHT_ROWS // 4
BIT = SLICE // 4
PARTS = ((144, 48), (0, 96), (96, 48))
SPATIAL_OFFSETS = tuple((dy, dx) for dy in (-1, 0, 1) for dx in (-1, 0, 1))
TEMPORAL_OFFSETS = (-1, 0, 1)
F32 = jnp.float32
BF16 = jnp.bfloat16


def group_values(first, second):
    rest = jnp.zeros((4, HALF), F32)
    rows = [first[:, :HALF], first[:, HALF:], second[:, :HALF], second[:, HALF:], rest]
    value = jnp.concatenate(rows, axis=0)
    place = lax.broadcasted_iota(jnp.int32, value.shape, 1) % 8
    values = [value]
    for step in range(1, 8):
        ahead = pltpu.roll(value, HALF - step, axis=1)
        back = pltpu.roll(value, 8 - step, axis=1)
        values.append(jnp.where(place < 8 - step, ahead, back))
    return values


def added(values):
    while len(values) > 1:
        values = [a + b for a, b in zip(values[::2], values[1::2])]
    return values[0]


def widened(rows):
    return jnp.concatenate([rows[0:1], rows[1:2]], axis=1)


def group_statistics(inputs):
    column = jnp.sum(inputs, axis=0, keepdims=True) * (1.0 / CELLS)
    within = inputs - column
    spread = jnp.sum(within * within, axis=0, keepdims=True) * (1.0 / CELLS)
    values = group_values(column, spread)
    mean = added(values) * 0.125
    between = added([(value - mean) * (value - mean) for value in values]) * 0.125
    scaling = lax.rsqrt(mean[2:4] + between[0:2] + EPSILON)
    return widened(mean[0:2]), widened(scaling)


def group_means(first, second):
    mean = added(group_values(first, second)) * (0.125 / CELLS)
    return widened(mean[0:2]), widened(mean[2:4])


def shift_x(value, dx):
    if dx == 0:
        return value
    lines = value.reshape(32, 8, CH)
    moved = pltpu.roll(lines, (-dx) % 8, axis=1)
    column = lax.broadcasted_iota(jnp.int32, lines.shape, 1)
    inside = column != (7 if dx == 1 else 0)
    return jnp.where(inside, moved, 0.0).reshape(CELLS, CH)


def shift_y(value, dy):
    if dy == 0:
        return value
    frames = value.reshape(4, 64, CH)
    edge = jnp.zeros((4, 8, CH), value.dtype)
    if dy == 1:
        frames = jnp.concatenate([frames[:, 8:], edge], axis=1)
    else:
        frames = jnp.concatenate([edge, frames[:, :56]], axis=1)
    return frames.reshape(CELLS, CH)


def shift_t(value, dt):
    if dt == 0:
        return value
    edge = jnp.zeros((64, CH), value.dtype)
    if dt == 1:
        return jnp.concatenate([value[64:], edge], axis=0)
    return jnp.concatenate([edge, value[:192]], axis=0)


def fill_spatial(cols, value, sign):
    for dx in (-1, 0, 1):
        moved = shift_x(value, sign * dx)
        for dy in (-1, 0, 1):
            tap = SPATIAL_OFFSETS.index((dy, dx))
            cols[:, tap * CH : (tap + 1) * CH] = shift_y(moved, sign * dy).astype(BF16)


def fill_temporal(cols, value, sign):
    for tap, dt in enumerate(TEMPORAL_OFFSETS):
        cols[:, tap * CH : (tap + 1) * CH] = shift_t(value, sign * dt)


def times_transposed(left, right):
    return lax.dot_general(left, right, (((1,), (1,)), ((), ())), preferred_element_type=F32)


def kernel(
    latents, cotangent, gain_ref, shift_ref, spatial_ref, temporal_ref,
    packed_out,
    wall, prm, hist, ghist, normed_s, slope_s, scale_s, cols, tcols, act_t, mid_t,
    gsend, first_in, first_sum, second_in, third_f, third_out, third_in, norm_acc,
    local_sem, own_send, own_recv, z_send, z_recv, relay_send, line_send, line_recv,
    mid_send, mid_recv, last_send, last_recv, far_send, far_recv, core_send, core_recv,
    prm_send, prm_recv, prm_core_send, prm_core_recv,
    g1_send, g1_recv, g2_send, g2_recv, g3_send, g3_recv, n_send, n_recv,
):
    dp = lax.axis_index("dp")
    pos = lax.axis_index("section")
    px = dp // 16
    py = (dp // 4) % 4
    pz = dp % 4
    block = pos // 2
    core = pos % 2

    def at_x(x):
        return (x * 16 + py * 4 + pz, pos)

    def at_y(y):
        return (px * 16 + y * 4 + pz, pos)

    def at_z(z):
        return (px * 16 + py * 4 + z, pos)

    def at_section(s):
        return (dp, s)

    def copy(src, dst, send, recv, device):
        return pltpu.make_async_remote_copy(
            src_ref=src, dst_ref=dst, send_sem=send, recv_sem=recv,
            device_id=device, device_id_type=MESH,
        )

    along = ((px, at_x), (py, at_y))

    barrier = pltpu.get_barrier_semaphore()
    for d in (1, 2, 3):
        for mine, place in along + ((pz, at_z),):
            pl.semaphore_signal(
                barrier, inc=1, device_id=place((mine + d) % 4), device_id_type=MESH
            )
    for other in (pos + 2, pos + 6, pos + 1 - 2 * core):
        pl.semaphore_signal(
            barrier, inc=1, device_id=at_section(other % 8), device_id_type=MESH
        )

    loads = [
        pltpu.make_async_copy(spatial_ref.at[0], wall.at[pos, pl.ds(0, SPATIAL)], local_sem.at[0]),
        pltpu.make_async_copy(
            temporal_ref.at[0], wall.at[pos, pl.ds(SPATIAL, WEIGHT_ROWS - SPATIAL)], local_sem.at[1]
        ),
        pltpu.make_async_copy(latents, hist.at[0], local_sem.at[2]),
        pltpu.make_async_copy(cotangent, ghist.at[8], local_sem.at[3]),
    ]
    for load in loads:
        load.start()
    rest = jnp.zeros((6, CH), F32)
    prm[pos] = jnp.concatenate([gain_ref[...], shift_ref[...], rest], axis=0)
    for load in loads:
        load.wait()
    pl.semaphore_wait(barrier, 12)

    other_core = at_section(pos + 1 - 2 * core)
    after = (block + 1) % 4
    behind = (block + 3) % 4

    def order(pair, seen_from):
        return jnp.where(pair < seen_from, pair, pair - 1)

    def pair_of(k):
        return jnp.where(k < block, k, k + 1)

    def section_of(k):
        return 2 * pair_of(k) + core

    def part(section, row, rows, half):
        return wall.at[section, pl.ds(row, rows), pl.ds(half * HALF, HALF)]

    def slice_row(m, n):
        return (n * 4 + m) * SLICE

    def own_copy():
        return copy(wall.at[pos], wall.at[pos], own_send.at[0], own_recv.at[0], other_core)

    def own_arrival():
        ref = wall.at[pos + 1 - 2 * core]
        return copy(ref, ref, own_send.at[0], own_recv.at[0], other_core)

    def bit(section, half, line):
        m, n = along[half][0], along[1 - half][0]
        return part(section, slice_row(m, n) + line * BIT, BIT, half)

    targets = (after, behind)

    def z_copy(way, half):
        target = targets[way]
        ref = bit(pos, half, pz)
        return copy(
            ref, ref, z_send.at[way, half], z_recv.at[order(block, target), half],
            at_section(target * 2 + core),
        )

    def z_arrival(k, half):
        ref = bit(section_of(k), half, pz)
        return copy(ref, ref, z_send.at[0, half], z_recv.at[k, half], at_section(after * 2 + core))

    def relay_copy(way):
        pair, target = (behind, after) if way == 0 else (after, behind)
        ref = bit(2 * pair + core, way, pz)
        return copy(
            ref, ref, relay_send.at[way], z_recv.at[order(pair, target), way],
            at_section(target * 2 + core),
        )

    def prm_copy(way):
        section = 2 * behind + core if way == 2 else pos
        target = after if way == 2 else targets[way]
        pair = behind if way == 2 else block
        return copy(
            prm.at[section], prm.at[section], prm_send.at[way], prm_recv.at[order(pair, target)],
            at_section(target * 2 + core),
        )

    def prm_arrival(k):
        ref = prm.at[section_of(k)]
        return copy(ref, ref, prm_send.at[0], prm_recv.at[k], at_section(after * 2 + core))

    def prm_core_copy(pair):
        ref = prm.at[2 * pair + core]
        return copy(ref, ref, prm_core_send.at[pair], prm_core_recv.at[pair], other_core)

    def prm_core_arrival(pair):
        ref = prm.at[2 * pair + 1 - core]
        return copy(ref, ref, prm_core_send.at[pair], prm_core_recv.at[pair], other_core)

    def line_copy(k, half, d):
        ref = bit(section_of(k), half, pz)
        return copy(
            ref, ref, line_send.at[k, half, d], line_recv.at[k, half, pz], at_z((pz + d) % 4)
        )

    def line_arrival(k, half, d):
        source = (pz + d) % 4
        ref = bit(section_of(k), half, source)
        return copy(ref, ref, line_send.at[k, half, d], line_recv.at[k, half, source], at_z(source))

    def mid_copy(k, half, slot, arrival=False):
        (m, place), n = along[half], along[1 - half][0]
        step = 1 if slot % 2 == 0 else 3
        if arrival:
            step = 4 - step
        target = place((m + step) % 4)
        if slot < 2:
            source = (m + step) % 4 if arrival else m
            row, rows = slice_row(source, n), SLICE
        else:
            source = (m + 2) % 4 if arrival else (m + 4 - step) % 4
            row, rows = slice_row(source, n) + (slot - 2) * (SLICE // 2), SLICE // 2
        ref = part(section_of(k), row, rows, half)
        return copy(ref, ref, mid_send.at[k, half, slot], mid_recv.at[k, half, slot], target)

    def last_copy(k, half, way, index, arrival=False):
        m, (n, place) = along[half][0], along[1 - half]
        step = 1 if way == 0 else 3
        if arrival:
            step = 4 - step
        slab = (n + step) % 4 if arrival else n
        row = slice_row((m + (0, 3, 1, 2)[index]) % 4, slab)
        ref = part(section_of(k), row, SLICE, half)
        return copy(
            ref, ref, last_send.at[k, half, way, index], last_recv.at[k, half, way, index],
            place((n + step) % 4),
        )

    def far_copy(k, half, index, arrival=False):
        m, (n, place) = along[half][0], along[1 - half]
        step = 1 if index < 2 else 3
        if arrival:
            step = 4 - step
        slab = (n + 2) % 4 if arrival else (n + 4 - step) % 4
        row = slice_row((m + (0, 3, 1, 2)[index]) % 4, slab)
        ref = part(section_of(k), row, SLICE, half)
        return copy(
            ref, ref, far_send.at[k, half, index], far_recv.at[k, half, index],
            place((n + step) % 4),
        )

    def core_copy(k, half, index, arrival=False):
        n = along[1 - half][0]
        section = 2 * pair_of(k) + (1 - core if arrival else core)
        ref = part(section, ((n + (0, 3, 1, 2)[index]) % 4) * LONG, LONG, half)
        return copy(
            ref, ref, core_send.at[k, half, index], core_recv.at[k, half, index], other_core
        )

    def relay_first():
        z_arrival(order(behind, block), 0).wait_recv()
        relay_copy(0).start()
        z_arrival(order(after, block), 1).wait_recv()
        relay_copy(1).start()

    def act_a(pair, relay):
        k = order(pair, block)
        for half in (0, 1):
            if relay != half:
                z_arrival(k, half).wait_recv()
            for d in (1, 3, 2):
                line_copy(k, half, d).start()
        prm_arrival(k).wait_recv()
        if relay == 0:
            prm_copy(2).start()
        prm_core_copy(pair).start()

    def act_b(k):
        for half in (0, 1):
            for d in (1, 3, 2):
                line_arrival(k, half, d).wait_recv()
            for slot in (0, 1):
                mid_copy(k, half, slot).start()
            for way in (0, 1):
                last_copy(k, half, way, 0).start()

    def act_c(k):
        for half in (0, 1):
            for slot in (0, 1):
                mid_copy(k, half, slot, True).wait_recv()
            for slot in (2, 3):
                mid_copy(k, half, slot).start()
            for index in (1, 2):
                for way in (0, 1):
                    last_copy(k, half, way, index).start()

    def act_d(k):
        for half in (0, 1):
            for slot in (2, 3):
                mid_copy(k, half, slot, True).wait_recv()
            for way in (0, 1):
                last_copy(k, half, way, 3).start()
            core_copy(k, half, 0).start()

    def act_e(k):
        for half in (0, 1):
            for index in (0, 1):
                last_copy(k, half, 0, index, True).wait_recv()
                far_copy(k, half, index).start()
            for index in (2, 3):
                last_copy(k, half, 1, index, True).wait_recv()
                far_copy(k, half, index).start()

    def act_f(k):
        for half in (0, 1):
            for index in (2, 3):
                last_copy(k, half, 0, index, True).wait_recv()
            core_copy(k, half, 1).start()
            for index in (0, 1):
                last_copy(k, half, 1, index, True).wait_recv()
            core_copy(k, half, 2).start()

    def act_g(k):
        for half in (0, 1):
            for index in range(4):
                far_copy(k, half, index, True).wait_recv()
            core_copy(k, half, 3).start()

    def act_h(k):
        for half in (0, 1):
            for index in range(4):
                core_copy(k, half, index, True).wait_recv()
        prm_core_arrival(pair_of(k)).wait_recv()

    for half in (0, 1):
        for way in (0, 1):
            z_copy(way, half).start()
    for way in (0, 1):
        prm_copy(way).start()
    prm_core_copy(block).start()
    own_copy().start()

    def gather_start():
        relay_first()
        act_a(behind, 0)
        act_a(after, 1)
        low = jnp.where(block == 2, 1, 0)
        high = jnp.where(block == 1, 1, 2)
        act_b(low)
        act_b(high)
        act_a((block + 2) % 4, None)
        act_b(3 - low - high)
        act_c(0)
        act_c(1)
        act_d(0)
        act_c(2)
        act_d(1)
        act_e(0)
        act_d(2)
        act_e(1)
        act_f(0)
        act_g(0)
        act_e(2)
        act_f(1)

    def gather_sent():
        def one(k, carry):
            for half in (0, 1):
                for d in (1, 3, 2):
                    line_copy(k, half, d).wait_send()
                for index in range(4):
                    mid_copy(k, half, index).wait_send()
                    for way in (0, 1):
                        last_copy(k, half, way, index).wait_send()
                    far_copy(k, half, index).wait_send()
                    core_copy(k, half, index).wait_send()
            return carry

        for half in (0, 1):
            for way in (0, 1):
                z_copy(way, half).wait_send()
            relay_copy(half).wait_send()
        for way in range(3):
            prm_copy(way).wait_send()
        for pair in range(4):
            prm_core_copy(pair).wait_send()
        own_copy().wait_send()
        lax.fori_loop(0, 3, one, 0)

    def forward(s):
        params = prm[s]
        gain = params[0:1]
        shift = params[1:2]
        decoder = s >= 4
        skip = jnp.where(decoder, 1.0, 0.0)
        inputs = hist[s].astype(F32) + skip * hist[jnp.where(decoder, 8 - s, 0)].astype(F32)
        center, scaling = group_statistics(inputs)
        normed = (inputs - center) * scaling
        before = normed * gain + shift
        sigma = jax.nn.sigmoid(before)
        normed_s[s] = normed
        slope_s[s] = sigma * (1.0 + before * (1.0 - sigma))
        scale_s[s] = jnp.broadcast_to(scaling, (8, CH))

        @pl.when((s < 7) | (pos == 7))
        def _():
            active = before * sigma
            fill_spatial(cols, active, 1)
            middle = jnp.dot(cols[...], wall[s, 0:SPATIAL], preferred_element_type=F32)
            rounded = middle.astype(BF16)
            fill_temporal(tcols, rounded, 1)
            branch = jnp.dot(tcols[...], wall[s, SPATIAL:WEIGHT_ROWS], preferred_element_type=F32)
            hist[s + 1] = (inputs + branch).astype(BF16)

            @pl.when(s == pos)
            def _():
                act_t[...] = active.T.astype(BF16)
                mid_t[...] = middle.T.astype(BF16)

    def forward_pair(pair, carry):
        foreign = pair != block
        k = order(pair, block)

        @pl.when(pair == jnp.where(block == 0, 1, 0))
        def _():
            gather_start()

        @pl.when(foreign)
        def _():
            act_h(k)

        @pl.when(pair == block)
        def _():
            own_arrival().wait_recv()
            prm_core_arrival(block).wait_recv()

        def one(index, inner):
            forward(2 * pair + index)

            @pl.when(foreign & (k == 0) & (index == 0))
            def _():
                act_g(1)
                act_f(2)

            @pl.when(foreign & (k == 0) & (index == 1))
            def _():
                act_g(2)

            return inner

        return lax.fori_loop(0, 2, one, carry)

    lax.fori_loop(0, 4, forward_pair, 0)

    def upstream(s):
        encoder = s < 4
        extra = jnp.where(encoder, 1.0, 0.0)
        other = ghist[jnp.where(encoder, 7 - s, 8)].astype(F32)
        return (ghist[s + 1].astype(F32) + extra * other).astype(BF16)

    def middle_grad(s):
        total = jnp.zeros((CELLS, CH), F32)
        for tap in range(3):
            weight = wall[s, SPATIAL + tap * CH : SPATIAL + (tap + 1) * CH]
            total = total + times_transposed(tcols[:, tap * CH : (tap + 1) * CH], weight)
        fill_spatial(cols, total, -1)

    def before_grad(s):
        total = jnp.zeros((CELLS, CH), F32)
        for tap in range(9):
            weight = wall[s, tap * CH : (tap + 1) * CH]
            total = total + times_transposed(cols[:, tap * CH : (tap + 1) * CH], weight)
        return total * slope_s[s]

    def backward(i, carry):
        s = 7 - i
        gain = prm[s][0:1]
        up = upstream(s)
        fill_temporal(tcols, up, -1)
        middle_grad(s)
        grad = before_grad(s)
        normed = normed_s[s]
        inner, project = group_means(
            gain * jnp.sum(grad, axis=0, keepdims=True),
            gain * jnp.sum(grad * normed, axis=0, keepdims=True),
        )
        input_grad = scale_s[s][0:1] * (grad * gain - inner - normed * project)
        ghist[s] = (up.astype(F32) + input_grad).astype(BF16)
        return carry

    lax.fori_loop(0, 7 - pos, backward, 0)

    def store_rows(tile, row, per_x, per_y, base):
        end = row + CH
        while row < end:
            stop = min(end, (row // per_y + 1) * per_y)
            where_x = row // per_x
            where_y = (row % per_x) // per_y
            inside = row % per_y
            start = CH - (end - row)
            gsend[where_x, where_y, base + inside : base + inside + stop - row, :] = tile[
                start : start + stop - row
            ]
            row = stop

    def own_part(half, index, sub):
        rows = pl.ds(*PARTS[sub])
        if half == 0:
            return gsend.at[index, :, rows, pl.ds(0, HALF)]
        return gsend.at[:, index, rows, pl.ds(HALF, HALF)]

    def g1_copy(half, sub, d, arrival=False):
        mine, place = along[half]
        other = (mine + d) % 4
        source = other if arrival else mine
        return copy(
            own_part(half, other, sub), first_in.at[half, source, :, pl.ds(*PARTS[sub])],
            g1_send.at[half, sub, d], g1_recv.at[half, sub, source], place(other),
        )

    def g1_start(sub):
        for half in (0, 1):
            for d in (1, 3, 2):
                g1_copy(half, sub, d).start()

    fill_temporal(tcols, upstream(pos), -1)
    for tap in range(3):
        tile = jnp.dot(mid_t[...], tcols[:, tap * CH : (tap + 1) * CH], preferred_element_type=F32)
        store_rows(tile.astype(BF16), tap * CH, 192, 48, 144)
    g1_start(0)
    middle_grad(pos)
    for tap in range(9):
        tile = jnp.dot(act_t[...], cols[:, tap * CH : (tap + 1) * CH], preferred_element_type=F32)
        store_rows(tile.astype(BF16), tap * CH, 576, 144, 0)

    def g2_copy(half, sub, d, arrival=False):
        mine, place = along[1 - half]
        other = (mine + d) % 4
        source = other if arrival else mine
        rows = pl.ds(*PARTS[sub])
        return copy(
            first_sum.at[half, other, rows], second_in.at[half, source, rows],
            g2_send.at[half, sub, d], g2_recv.at[half, sub, source], place(other),
        )

    def g3_copy(d):
        target = (pz + d) % 4
        return copy(
            third_out.at[target], third_in.at[pz], g3_send.at[d], g3_recv.at[pz], at_z(target)
        )

    def g3_arrival(d):
        source = (pz + d) % 4
        return copy(
            third_out.at[source], third_in.at[source], g3_send.at[d], g3_recv.at[source], at_z(source)
        )

    g1_start(1)
    g1_start(2)

    axes = along + ((pz, at_z),)

    def n_copy(phase, d):
        mine, place = axes[phase]
        return copy(
            norm_acc.at[phase, mine], norm_acc.at[phase, mine], n_send.at[phase, d],
            n_recv.at[phase, mine], place((mine + d) % 4),
        )

    def n_arrival(phase, d):
        mine, place = axes[phase]
        source = (mine + d) % 4
        return copy(
            norm_acc.at[phase, source], norm_acc.at[phase, source], n_send.at[phase, d],
            n_recv.at[phase, source], place(source),
        )

    grad = before_grad(pos)
    gain_term = jnp.sum(grad * normed_s[pos], axis=0, keepdims=True)
    shift_term = jnp.sum(grad, axis=0, keepdims=True)
    norm_value = jnp.concatenate([gain_term, shift_term, rest], axis=0)

    def norm_start(phase, value):
        norm_acc[phase, axes[phase][0]] = value
        for d in (1, 3, 2):
            n_copy(phase, d).start()

    def norm_finish(phase):
        for d in (1, 3, 2):
            n_arrival(phase, d).wait_recv()
        return ((norm_acc[phase, 0] + norm_acc[phase, 1]) + norm_acc[phase, 2]) + norm_acc[phase, 3]

    norm_start(0, norm_value)
    gather_sent()

    for sub in (0, 1, 2):
        for half in (0, 1):
            mine = along[half][0]
            rows = slice(PARTS[sub][0], sum(PARTS[sub]))
            for d in (1, 3, 2):
                g1_copy(half, sub, d, True).wait_recv()
            for index in range(4):
                if half == 0:
                    total = gsend[mine, index, rows, 0:HALF].astype(F32)
                else:
                    total = gsend[index, mine, rows, HALF:CH].astype(F32)
                for d in (1, 2, 3):
                    total = total + first_in[half, (mine + d) % 4, index, rows].astype(F32)
                first_sum[half, index, rows] = total.astype(BF16)
            for d in (1, 3, 2):
                g2_copy(half, sub, d).start()

    norm_start(1, norm_finish(0))

    for half in (0, 1):
        mine = along[1 - half][0]
        for sub in (0, 1, 2):
            for d in (1, 3, 2):
                g2_copy(half, sub, d, True).wait_recv()
        total = first_sum[half, mine].astype(F32)
        for d in (1, 2, 3):
            total = total + second_in[half, (mine + d) % 4].astype(F32)
        columns = slice(half * HALF, (half + 1) * HALF)
        for z in range(4):
            third_f[z, 0:36, columns] = total[z * 36 : (z + 1) * 36]
            third_f[z, 36:48, columns] = total[144 + z * 12 : 144 + (z + 1) * 12]
    for z in range(4):
        third_out[z] = third_f[z].astype(BF16)
    for d in (1, 3, 2):
        g3_copy(d).start()

    norm_start(2, norm_finish(1))

    total = third_f[pz]
    for d in (1, 3, 2):
        g3_arrival(d).wait_recv()
    for d in (1, 2, 3):
        total = total + third_in[(pz + d) % 4].astype(F32)
    packed_out[0:48] = total
    packed_out[48:56] = norm_finish(2)

    for d in (1, 3, 2):
        for half in (0, 1):
            for sub in (0, 1, 2):
                g1_copy(half, sub, d).wait_send()
                g2_copy(half, sub, d).wait_send()
        g3_copy(d).wait_send()
        for phase in range(3):
            n_copy(phase, d).wait_send()


def unpack(packed, spatial_out, temporal_out, norm_out):
    spatial_out[...] = packed[0:36].reshape(36, 1, CH)
    temporal_out[...] = packed[36:48].reshape(12, 1, CH)
    norm_out[0] = packed[48:50]


def shards(latents, cotangent, spatial_weight, temporal_weight, norm_gain, norm_shift):
    vmem = pl.BlockSpec(memory_space=pltpu.VMEM)
    anywhere = pl.BlockSpec(memory_space=pl.ANY)
    dma = pltpu.SemaphoreType.DMA
    packed = pl.pallas_call(
        kernel,
        out_shape=jax.ShapeDtypeStruct((56, CH), F32),
        in_specs=[anywhere, anywhere, vmem, vmem, anywhere, anywhere],
        out_specs=vmem,
        scratch_shapes=[
            pltpu.VMEM((8, WEIGHT_ROWS, CH), BF16),
            pltpu.VMEM((8, 8, CH), F32),
            pltpu.VMEM((9, CELLS, CH), BF16),
            pltpu.VMEM((9, CELLS, CH), BF16),
            pltpu.VMEM((8, CELLS, CH), F32),
            pltpu.VMEM((8, CELLS, CH), F32),
            pltpu.VMEM((8, 8, CH), F32),
            pltpu.VMEM((CELLS, SPATIAL), BF16),
            pltpu.VMEM((CELLS, 3 * CH), BF16),
            pltpu.VMEM((CH, CELLS), BF16),
            pltpu.VMEM((CH, CELLS), BF16),
            pltpu.VMEM((4, 4, 192, CH), BF16),
            pltpu.VMEM((2, 4, 4, 192, HALF), BF16),
            pltpu.VMEM((2, 4, 192, HALF), BF16),
            pltpu.VMEM((2, 4, 192, HALF), BF16),
            pltpu.VMEM((4, 48, CH), F32),
            pltpu.VMEM((4, 48, CH), BF16),
            pltpu.VMEM((4, 48, CH), BF16),
            pltpu.VMEM((3, 4, 8, CH), F32),
            dma((4,)),
            dma((1,)), dma((1,)),
            dma((2, 2)), dma((3, 2)), dma((2,)),
            dma((3, 2, 4)), dma((3, 2, 4)),
            dma((3, 2, 4)), dma((3, 2, 4)),
            dma((3, 2, 2, 4)), dma((3, 2, 2, 4)),
            dma((3, 2, 4)), dma((3, 2, 4)),
            dma((3, 2, 4)), dma((3, 2, 4)),
            dma((3,)), dma((3,)),
            dma((4,)), dma((4,)),
            dma((2, 3, 4)), dma((2, 3, 4)),
            dma((2, 3, 4)), dma((2, 3, 4)),
            dma((4,)), dma((4,)),
            dma((3, 4)), dma((3, 4)),
        ],
        compiler_params=pltpu.CompilerParams(
            collective_id=0, has_side_effects=True, vmem_limit_bytes=56 * 1024 * 1024
        ),
        cost_estimate=pl.CostEstimate(
            flops=2 * 256 * 256 * 3072 * 17, bytes_accessed=4 * 1024 * 1024, transcendentals=8 * 65536
        ),
    )(
        latents.reshape(CELLS, CH), cotangent.reshape(CELLS, CH), norm_gain, norm_shift,
        spatial_weight, temporal_weight,
    )
    spatial, temporal, norm = pl.pallas_call(
        unpack,
        out_shape=(
            jax.ShapeDtypeStruct((36, 1, CH), F32),
            jax.ShapeDtypeStruct((12, 1, CH), F32),
            jax.ShapeDtypeStruct((1, 2, CH), F32),
        ),
        in_specs=[vmem],
        out_specs=(vmem, vmem, vmem),
    )(packed)
    return (spatial.transpose(1, 0, 2), temporal.transpose(1, 0, 2), norm)


def solution(mesh):
    return jax.shard_map(
        shards,
        mesh=mesh,
        in_specs=(
            P("dp", None, None, None, None),
            P("dp", None, None, None, None),
            P("section", None, None),
            P("section", None, None),
            P("section", None),
            P("section", None),
        ),
        out_specs=(P("section", "dp", None), P("section", "dp", None), P("section", None, None)),
        check_vma=False,
    )
```

```python
import functools

import jax
import jax.numpy as jnp
from jax import lax
from jax.experimental import pallas as pl
from jax.experimental.pallas import tpu as pltpu
from jax.sharding import PartitionSpec as P

MESH = pl.DeviceIdType.MESH
EPSILON = 1e-05
CELLS = 256
CH = 256
HALF = 128
SPATIAL = 2304
WEIGHT_ROWS = 3072
SLICE = WEIGHT_ROWS // 16
LONG = WEIGHT_ROWS // 4
BIT = SLICE // 4
PARTS = ((144, 48), (0, 96), (96, 48))
SPATIAL_OFFSETS = tuple((dy, dx) for dy in (-1, 0, 1) for dx in (-1, 0, 1))
TEMPORAL_OFFSETS = (-1, 0, 1)
F32 = jnp.float32
BF16 = jnp.bfloat16


def group_values(first, second):
    rest = jnp.zeros((4, HALF), F32)
    rows = [first[:, :HALF], first[:, HALF:], second[:, :HALF], second[:, HALF:], rest]
    value = jnp.concatenate(rows, axis=0)
    place = lax.broadcasted_iota(jnp.int32, value.shape, 1) % 8
    values = [value]
    for step in range(1, 8):
        ahead = pltpu.roll(value, HALF - step, axis=1)
        back = pltpu.roll(value, 8 - step, axis=1)
        values.append(jnp.where(place < 8 - step, ahead, back))
    return values


def added(values):
    while len(values) > 1:
        values = [a + b for a, b in zip(values[::2], values[1::2])]
    return values[0]


def widened(rows):
    return jnp.concatenate([rows[0:1], rows[1:2]], axis=1)


def group_statistics(inputs):
    column = jnp.sum(inputs, axis=0, keepdims=True) * (1.0 / CELLS)
    within = inputs - column
    spread = jnp.sum(within * within, axis=0, keepdims=True) * (1.0 / CELLS)
    values = group_values(column, spread)
    mean = added(values) * 0.125
    between = added([(value - mean) * (value - mean) for value in values]) * 0.125
    scaling = lax.rsqrt(mean[2:4] + between[0:2] + EPSILON)
    return widened(mean[0:2]), widened(scaling)


def group_means(first, second):
    mean = added(group_values(first, second)) * (0.125 / CELLS)
    return widened(mean[0:2]), widened(mean[2:4])


def shift_x(value, dx):
    if dx == 0:
        return value
    lines = value.reshape(32, 8, CH)
    moved = pltpu.roll(lines, (-dx) % 8, axis=1)
    column = lax.broadcasted_iota(jnp.int32, lines.shape, 1)
    inside = column != (7 if dx == 1 else 0)
    return jnp.where(inside, moved, 0.0).reshape(CELLS, CH)


def shift_y(value, dy):
    if dy == 0:
        return value
    frames = value.reshape(4, 64, CH)
    edge = jnp.zeros((4, 8, CH), value.dtype)
    if dy == 1:
        frames = jnp.concatenate([frames[:, 8:], edge], axis=1)
    else:
        frames = jnp.concatenate([edge, frames[:, :56]], axis=1)
    return frames.reshape(CELLS, CH)


def shift_t(value, dt):
    if dt == 0:
        return value
    edge = jnp.zeros((64, CH), value.dtype)
    if dt == 1:
        return jnp.concatenate([value[64:], edge], axis=0)
    return jnp.concatenate([edge, value[:192]], axis=0)


def fill_spatial(cols, value, sign):
    for dx in (-1, 0, 1):
        moved = shift_x(value, sign * dx)
        for dy in (-1, 0, 1):
            tap = SPATIAL_OFFSETS.index((dy, dx))
            cols[:, tap * CH : (tap + 1) * CH] = shift_y(moved, sign * dy).astype(BF16)


def fill_temporal(cols, value, sign):
    for tap, dt in enumerate(TEMPORAL_OFFSETS):
        cols[:, tap * CH : (tap + 1) * CH] = shift_t(value, sign * dt)


def times_transposed(left, right):
    return lax.dot_general(left, right, (((1,), (1,)), ((), ())), preferred_element_type=F32)


def kernel(
    latents, cotangent, gain_ref, shift_ref, spatial_ref, temporal_ref,
    packed_out,
    wall, prm, hist, ghist, normed_s, slope_s, scale_s, cols, tcols, act_t, mid_t,
    gsend, first_in, first_sum, second_in, third_f, third_out, third_in, norm_acc,
    local_sem, own_send, own_recv, z_send, z_recv, relay_send, line_send, line_recv,
    mid_send, mid_recv, last_send, last_recv, far_send, far_recv, core_send, core_recv,
    prm_send, prm_recv, prm_core_send, prm_core_recv,
    g1_send, g1_recv, g2_send, g2_recv, g3_send, g3_recv, n_send, n_recv,
):
    dp = lax.axis_index("dp")
    pos = lax.axis_index("section")
    px = dp // 16
    py = (dp // 4) % 4
    pz = dp % 4
    block = pos // 2
    core = pos % 2

    def at_x(x):
        return (x * 16 + py * 4 + pz, pos)

    def at_y(y):
        return (px * 16 + y * 4 + pz, pos)

    def at_z(z):
        return (px * 16 + py * 4 + z, pos)

    def at_section(s):
        return (dp, s)

    def copy(src, dst, send, recv, device):
        return pltpu.make_async_remote_copy(
            src_ref=src, dst_ref=dst, send_sem=send, recv_sem=recv,
            device_id=device, device_id_type=MESH,
        )

    along = ((px, at_x), (py, at_y))

    barrier = pltpu.get_barrier_semaphore()
    for d in (1, 2, 3):
        for mine, place in along + ((pz, at_z),):
            pl.semaphore_signal(
                barrier, inc=1, device_id=place((mine + d) % 4), device_id_type=MESH
            )
    for other in (pos + 2, pos + 6, pos + 1 - 2 * core):
        pl.semaphore_signal(
            barrier, inc=1, device_id=at_section(other % 8), device_id_type=MESH
        )

    loads = [
        pltpu.make_async_copy(spatial_ref.at[0], wall.at[pos, pl.ds(0, SPATIAL)], local_sem.at[0]),
        pltpu.make_async_copy(
            temporal_ref.at[0], wall.at[pos, pl.ds(SPATIAL, WEIGHT_ROWS - SPATIAL)], local_sem.at[1]
        ),
        pltpu.make_async_copy(latents, hist.at[0], local_sem.at[2]),
        pltpu.make_async_copy(cotangent, ghist.at[8], local_sem.at[3]),
    ]
    for load in loads:
        load.start()
    rest = jnp.zeros((6, CH), F32)
    prm[pos] = jnp.concatenate([gain_ref[...], shift_ref[...], rest], axis=0)
    for load in loads:
        load.wait()
    pl.semaphore_wait(barrier, 12)

    other_core = at_section(pos + 1 - 2 * core)
    after = (block + 1) % 4
    behind = (block + 3) % 4

    def order(pair, seen_from):
        return jnp.where(pair < seen_from, pair, pair - 1)

    def pair_of(k):
        return jnp.where(k < block, k, k + 1)

    def section_of(k):
        return 2 * pair_of(k) + core

    def part(section, row, rows, half):
        return wall.at[section, pl.ds(row, rows), pl.ds(half * HALF, HALF)]

    def slice_row(m, n):
        return (n * 4 + m) * SLICE

    def own_copy():
        return copy(wall.at[pos], wall.at[pos], own_send.at[0], own_recv.at[0], other_core)

    def own_arrival():
        ref = wall.at[pos + 1 - 2 * core]
        return copy(ref, ref, own_send.at[0], own_recv.at[0], other_core)

    def bit(section, half, line):
        m, n = along[half][0], along[1 - half][0]
        return part(section, slice_row(m, n) + line * BIT, BIT, half)

    targets = (after, behind)

    def z_copy(way, half):
        target = targets[way]
        ref = bit(pos, half, pz)
        return copy(
            ref, ref, z_send.at[way, half], z_recv.at[order(block, target), half],
            at_section(target * 2 + core),
        )

    def z_arrival(k, half):
        ref = bit(section_of(k), half, pz)
        return copy(ref, ref, z_send.at[0, half], z_recv.at[k, half], at_section(after * 2 + core))

    def relay_copy(way):
        pair, target = (behind, after) if way == 0 else (after, behind)
        ref = bit(2 * pair + core, way, pz)
        return copy(
            ref, ref, relay_send.at[way], z_recv.at[order(pair, target), way],
            at_section(target * 2 + core),
        )

    def prm_copy(way):
        section = 2 * behind + core if way == 2 else pos
        target = after if way == 2 else targets[way]
        pair = behind if way == 2 else block
        return copy(
            prm.at[section], prm.at[section], prm_send.at[way], prm_recv.at[order(pair, target)],
            at_section(target * 2 + core),
        )

    def prm_arrival(k):
        ref = prm.at[section_of(k)]
        return copy(ref, ref, prm_send.at[0], prm_recv.at[k], at_section(after * 2 + core))

    def prm_core_copy(pair):
        ref = prm.at[2 * pair + core]
        return copy(ref, ref, prm_core_send.at[pair], prm_core_recv.at[pair], other_core)

    def prm_core_arrival(pair):
        ref = prm.at[2 * pair + 1 - core]
        return copy(ref, ref, prm_core_send.at[pair], prm_core_recv.at[pair], other_core)

    def line_copy(k, half, d):
        ref = bit(section_of(k), half, pz)
        return copy(
            ref, ref, line_send.at[k, half, d], line_recv.at[k, half, pz], at_z((pz + d) % 4)
        )

    def line_arrival(k, half, d):
        source = (pz + d) % 4
        ref = bit(section_of(k), half, source)
        return copy(ref, ref, line_send.at[k, half, d], line_recv.at[k, half, source], at_z(source))

    def mid_copy(k, half, slot, arrival=False):
        (m, place), n = along[half], along[1 - half][0]
        step = 1 if slot % 2 == 0 else 3
        if arrival:
            step = 4 - step
        target = place((m + step) % 4)
        if slot < 2:
            source = (m + step) % 4 if arrival else m
            row, rows = slice_row(source, n), SLICE
        else:
            source = (m + 2) % 4 if arrival else (m + 4 - step) % 4
            row, rows = slice_row(source, n) + (slot - 2) * (SLICE // 2), SLICE // 2
        ref = part(section_of(k), row, rows, half)
        return copy(ref, ref, mid_send.at[k, half, slot], mid_recv.at[k, half, slot], target)

    def last_copy(k, half, way, index, arrival=False):
        m, (n, place) = along[half][0], along[1 - half]
        step = 1 if way == 0 else 3
        if arrival:
            step = 4 - step
        slab = (n + step) % 4 if arrival else n
        row = slice_row((m + (0, 3, 1, 2)[index]) % 4, slab)
        ref = part(section_of(k), row, SLICE, half)
        return copy(
            ref, ref, last_send.at[k, half, way, index], last_recv.at[k, half, way, index],
            place((n + step) % 4),
        )

    def far_copy(k, half, index, arrival=False):
        m, (n, place) = along[half][0], along[1 - half]
        step = 1 if index < 2 else 3
        if arrival:
            step = 4 - step
        slab = (n + 2) % 4 if arrival else (n + 4 - step) % 4
        row = slice_row((m + (0, 3, 1, 2)[index]) % 4, slab)
        ref = part(section_of(k), row, SLICE, half)
        return copy(
            ref, ref, far_send.at[k, half, index], far_recv.at[k, half, index],
            place((n + step) % 4),
        )

    def core_copy(k, half, index, arrival=False):
        n = along[1 - half][0]
        section = 2 * pair_of(k) + (1 - core if arrival else core)
        ref = part(section, ((n + (0, 3, 1, 2)[index]) % 4) * LONG, LONG, half)
        return copy(
            ref, ref, core_send.at[k, half, index], core_recv.at[k, half, index], other_core
        )

    def relay_first():
        z_arrival(order(behind, block), 0).wait_recv()
        relay_copy(0).start()
        z_arrival(order(after, block), 1).wait_recv()
        relay_copy(1).start()

    def act_a(pair, relay):
        k = order(pair, block)
        for half in (0, 1):
            if relay != half:
                z_arrival(k, half).wait_recv()
            for d in (1, 3, 2):
                line_copy(k, half, d).start()
        prm_arrival(k).wait_recv()
        if relay == 0:
            prm_copy(2).start()
        prm_core_copy(pair).start()

    def act_b(k):
        for half in (0, 1):
            for d in (1, 3, 2):
                line_arrival(k, half, d).wait_recv()
            for slot in (0, 1):
                mid_copy(k, half, slot).start()
            for way in (0, 1):
                last_copy(k, half, way, 0).start()

    def act_c(k):
        for half in (0, 1):
            for slot in (0, 1):
                mid_copy(k, half, slot, True).wait_recv()
            for slot in (2, 3):
                mid_copy(k, half, slot).start()
            for index in (1, 2):
                for way in (0, 1):
                    last_copy(k, half, way, index).start()

    def act_d(k):
        for half in (0, 1):
            for slot in (2, 3):
                mid_copy(k, half, slot, True).wait_recv()
            for way in (0, 1):
                last_copy(k, half, way, 3).start()
            core_copy(k, half, 0).start()

    def act_e(k):
        for half in (0, 1):
            for index in (0, 1):
                last_copy(k, half, 0, index, True).wait_recv()
                far_copy(k, half, index).start()
            for index in (2, 3):
                last_copy(k, half, 1, index, True).wait_recv()
                far_copy(k, half, index).start()

    def act_f(k):
        for half in (0, 1):
            for index in (2, 3):
                last_copy(k, half, 0, index, True).wait_recv()
            core_copy(k, half, 1).start()
            for index in (0, 1):
                last_copy(k, half, 1, index, True).wait_recv()
            core_copy(k, half, 2).start()

    def act_g(k):
        for half in (0, 1):
            for index in range(4):
                far_copy(k, half, index, True).wait_recv()
            core_copy(k, half, 3).start()

    def act_h(k):
        for half in (0, 1):
            for index in range(4):
                core_copy(k, half, index, True).wait_recv()
        prm_core_arrival(pair_of(k)).wait_recv()

    for half in (0, 1):
        for way in (0, 1):
            z_copy(way, half).start()
    for way in (0, 1):
        prm_copy(way).start()
    prm_core_copy(block).start()
    own_copy().start()

    def gather_start():
        relay_first()
        act_a(behind, 0)
        act_a(after, 1)
        low = jnp.where(block == 2, 1, 0)
        high = jnp.where(block == 1, 1, 2)
        act_b(low)
        act_b(high)
        act_a((block + 2) % 4, None)
        act_b(3 - low - high)
        act_c(0)
        act_c(1)
        act_d(0)
        act_c(2)
        act_d(1)
        act_e(0)
        act_d(2)
        act_e(1)
        act_f(0)
        act_g(0)
        act_e(2)
        act_f(1)
        act_f(2)

    def gather_sent():
        def one(k, carry):
            for half in (0, 1):
                for d in (1, 3, 2):
                    line_copy(k, half, d).wait_send()
                for index in range(4):
                    mid_copy(k, half, index).wait_send()
                    for way in (0, 1):
                        last_copy(k, half, way, index).wait_send()
                    far_copy(k, half, index).wait_send()
                    core_copy(k, half, index).wait_send()
            return carry

        for half in (0, 1):
            for way in (0, 1):
                z_copy(way, half).wait_send()
            relay_copy(half).wait_send()
        for way in range(3):
            prm_copy(way).wait_send()
        for pair in range(4):
            prm_core_copy(pair).wait_send()
        own_copy().wait_send()
        lax.fori_loop(0, 3, one, 0)

    def forward(s):
        params = prm[s]
        gain = params[0:1]
        shift = params[1:2]
        decoder = s >= 4
        skip = jnp.where(decoder, 1.0, 0.0)
        inputs = hist[s].astype(F32) + skip * hist[jnp.where(decoder, 8 - s, 0)].astype(F32)
        center, scaling = group_statistics(inputs)
        normed = (inputs - center) * scaling
        before = normed * gain + shift
        sigma = jax.nn.sigmoid(before)
        normed_s[s] = normed
        slope_s[s] = sigma * (1.0 + before * (1.0 - sigma))
        scale_s[s] = jnp.broadcast_to(scaling, (8, CH))

        @pl.when((s < 7) | (pos == 7))
        def _():
            active = before * sigma
            fill_spatial(cols, active, 1)
            middle = jnp.dot(cols[...], wall[s, 0:SPATIAL], preferred_element_type=F32)
            rounded = middle.astype(BF16)
            fill_temporal(tcols, rounded, 1)
            branch = jnp.dot(tcols[...], wall[s, SPATIAL:WEIGHT_ROWS], preferred_element_type=F32)
            hist[s + 1] = (inputs + branch).astype(BF16)

            @pl.when(s == pos)
            def _():
                act_t[...] = active.T.astype(BF16)
                mid_t[...] = middle.T.astype(BF16)

    def forward_pair(pair, carry):
        foreign = pair != block
        k = order(pair, block)

        @pl.when(pair == jnp.where(block == 0, 1, 0))
        def _():
            gather_start()

        @pl.when(foreign)
        def _():
            act_h(k)

        @pl.when(pair == block)
        def _():
            own_arrival().wait_recv()
            prm_core_arrival(block).wait_recv()

        def one(index, inner):
            forward(2 * pair + index)

            @pl.when(foreign & (k == 0) & (index == 0))
            def _():
                act_g(1)

            @pl.when(foreign & (k == 0) & (index == 1))
            def _():
                act_g(2)

            return inner

        return lax.fori_loop(0, 2, one, carry)

    lax.fori_loop(0, 4, forward_pair, 0)

    def upstream(s):
        encoder = s < 4
        extra = jnp.where(encoder, 1.0, 0.0)
        other = ghist[jnp.where(encoder, 7 - s, 8)].astype(F32)
        return (ghist[s + 1].astype(F32) + extra * other).astype(BF16)

    def middle_grad(s):
        total = jnp.zeros((CELLS, CH), F32)
        for tap in range(3):
            weight = wall[s, SPATIAL + tap * CH : SPATIAL + (tap + 1) * CH]
            total = total + times_transposed(tcols[:, tap * CH : (tap + 1) * CH], weight)
        fill_spatial(cols, total, -1)

    def before_grad(s):
        total = jnp.zeros((CELLS, CH), F32)
        for tap in range(9):
            weight = wall[s, tap * CH : (tap + 1) * CH]
            total = total + times_transposed(cols[:, tap * CH : (tap + 1) * CH], weight)
        return total * slope_s[s]

    def backward(i, carry):
        s = 7 - i
        gain = prm[s][0:1]
        up = upstream(s)
        fill_temporal(tcols, up, -1)
        middle_grad(s)
        grad = before_grad(s)
        normed = normed_s[s]
        inner, project = group_means(
            gain * jnp.sum(grad, axis=0, keepdims=True),
            gain * jnp.sum(grad * normed, axis=0, keepdims=True),
        )
        input_grad = scale_s[s][0:1] * (grad * gain - inner - normed * project)
        ghist[s] = (up.astype(F32) + input_grad).astype(BF16)
        return carry

    lax.fori_loop(0, 7 - pos, backward, 0)

    def store_rows(tile, row, per_x, per_y, base):
        end = row + CH
        while row < end:
            stop = min(end, (row // per_y + 1) * per_y)
            where_x = row // per_x
            where_y = (row % per_x) // per_y
            inside = row % per_y
            start = CH - (end - row)
            gsend[where_x, where_y, base + inside : base + inside + stop - row, :] = tile[
                start : start + stop - row
            ]
            row = stop

    def own_part(half, index, sub):
        rows = pl.ds(*PARTS[sub])
        if half == 0:
            return gsend.at[index, :, rows, pl.ds(0, HALF)]
        return gsend.at[:, index, rows, pl.ds(HALF, HALF)]

    def g1_copy(half, sub, d, arrival=False):
        mine, place = along[half]
        other = (mine + d) % 4
        source = other if arrival else mine
        return copy(
            own_part(half, other, sub), first_in.at[half, source, :, pl.ds(*PARTS[sub])],
            g1_send.at[half, sub, d], g1_recv.at[half, sub, source], place(other),
        )

    def g1_start(sub):
        for half in (0, 1):
            for d in (1, 3, 2):
                g1_copy(half, sub, d).start()

    fill_temporal(tcols, upstream(pos), -1)
    for tap in range(3):
        tile = jnp.dot(mid_t[...], tcols[:, tap * CH : (tap + 1) * CH], preferred_element_type=F32)
        store_rows(tile.astype(BF16), tap * CH, 192, 48, 144)
    g1_start(0)
    middle_grad(pos)
    for tap in range(9):
        tile = jnp.dot(act_t[...], cols[:, tap * CH : (tap + 1) * CH], preferred_element_type=F32)
        store_rows(tile.astype(BF16), tap * CH, 576, 144, 0)

    def g2_copy(half, sub, d, arrival=False):
        mine, place = along[1 - half]
        other = (mine + d) % 4
        source = other if arrival else mine
        rows = pl.ds(*PARTS[sub])
        return copy(
            first_sum.at[half, other, rows], second_in.at[half, source, rows],
            g2_send.at[half, sub, d], g2_recv.at[half, sub, source], place(other),
        )

    def g3_copy(d):
        target = (pz + d) % 4
        return copy(
            third_out.at[target], third_in.at[pz], g3_send.at[d], g3_recv.at[pz], at_z(target)
        )

    def g3_arrival(d):
        source = (pz + d) % 4
        return copy(
            third_out.at[source], third_in.at[source], g3_send.at[d], g3_recv.at[source], at_z(source)
        )

    g1_start(1)
    g1_start(2)

    axes = along + ((pz, at_z),)

    def n_copy(phase, d):
        mine, place = axes[phase]
        return copy(
            norm_acc.at[phase, mine], norm_acc.at[phase, mine], n_send.at[phase, d],
            n_recv.at[phase, mine], place((mine + d) % 4),
        )

    def n_arrival(phase, d):
        mine, place = axes[phase]
        source = (mine + d) % 4
        return copy(
            norm_acc.at[phase, source], norm_acc.at[phase, source], n_send.at[phase, d],
            n_recv.at[phase, source], place(source),
        )

    grad = before_grad(pos)
    gain_term = jnp.sum(grad * normed_s[pos], axis=0, keepdims=True)
    shift_term = jnp.sum(grad, axis=0, keepdims=True)
    norm_value = jnp.concatenate([gain_term, shift_term, rest], axis=0)

    def norm_start(phase, value):
        norm_acc[phase, axes[phase][0]] = value
        for d in (1, 3, 2):
            n_copy(phase, d).start()

    def norm_finish(phase):
        for d in (1, 3, 2):
            n_arrival(phase, d).wait_recv()
        return ((norm_acc[phase, 0] + norm_acc[phase, 1]) + norm_acc[phase, 2]) + norm_acc[phase, 3]

    norm_start(0, norm_value)
    gather_sent()

    for sub in (0, 1, 2):
        for half in (0, 1):
            mine = along[half][0]
            rows = slice(PARTS[sub][0], sum(PARTS[sub]))
            for d in (1, 3, 2):
                g1_copy(half, sub, d, True).wait_recv()
            for index in range(4):
                if half == 0:
                    total = gsend[mine, index, rows, 0:HALF].astype(F32)
                else:
                    total = gsend[index, mine, rows, HALF:CH].astype(F32)
                for d in (1, 2, 3):
                    total = total + first_in[half, (mine + d) % 4, index, rows].astype(F32)
                first_sum[half, index, rows] = total.astype(BF16)
            for d in (1, 3, 2):
                g2_copy(half, sub, d).start()

    norm_start(1, norm_finish(0))

    for half in (0, 1):
        mine = along[1 - half][0]
        for sub in (0, 1, 2):
            for d in (1, 3, 2):
                g2_copy(half, sub, d, True).wait_recv()
        total = first_sum[half, mine].astype(F32)
        for d in (1, 2, 3):
            total = total + second_in[half, (mine + d) % 4].astype(F32)
        columns = slice(half * HALF, (half + 1) * HALF)
        for z in range(4):
            third_f[z, 0:36, columns] = total[z * 36 : (z + 1) * 36]
            third_f[z, 36:48, columns] = total[144 + z * 12 : 144 + (z + 1) * 12]
    for z in range(4):
        third_out[z] = third_f[z].astype(BF16)
    for d in (1, 3, 2):
        g3_copy(d).start()

    norm_start(2, norm_finish(1))

    total = third_f[pz]
    for d in (1, 3, 2):
        g3_arrival(d).wait_recv()
    for d in (1, 2, 3):
        total = total + third_in[(pz + d) % 4].astype(F32)
    packed_out[0:48] = total
    packed_out[48:56] = norm_finish(2)

    for d in (1, 3, 2):
        for half in (0, 1):
            for sub in (0, 1, 2):
                g1_copy(half, sub, d).wait_send()
                g2_copy(half, sub, d).wait_send()
        g3_copy(d).wait_send()
        for phase in range(3):
            n_copy(phase, d).wait_send()


def unpack(packed, spatial_out, temporal_out, norm_out):
    spatial_out[...] = packed[0:36].reshape(36, 1, CH)
    temporal_out[...] = packed[36:48].reshape(12, 1, CH)
    norm_out[0] = packed[48:50]


def shards(latents, cotangent, spatial_weight, temporal_weight, norm_gain, norm_shift):
    vmem = pl.BlockSpec(memory_space=pltpu.VMEM)
    anywhere = pl.BlockSpec(memory_space=pl.ANY)
    dma = pltpu.SemaphoreType.DMA
    packed = pl.pallas_call(
        kernel,
        out_shape=jax.ShapeDtypeStruct((56, CH), F32),
        in_specs=[anywhere, anywhere, vmem, vmem, anywhere, anywhere],
        out_specs=vmem,
        scratch_shapes=[
            pltpu.VMEM((8, WEIGHT_ROWS, CH), BF16),
            pltpu.VMEM((8, 8, CH), F32),
            pltpu.VMEM((9, CELLS, CH), BF16),
            pltpu.VMEM((9, CELLS, CH), BF16),
            pltpu.VMEM((8, CELLS, CH), F32),
            pltpu.VMEM((8, CELLS, CH), F32),
            pltpu.VMEM((8, 8, CH), F32),
            pltpu.VMEM((CELLS, SPATIAL), BF16),
            pltpu.VMEM((CELLS, 3 * CH), BF16),
            pltpu.VMEM((CH, CELLS), BF16),
            pltpu.VMEM((CH, CELLS), BF16),
            pltpu.VMEM((4, 4, 192, CH), BF16),
            pltpu.VMEM((2, 4, 4, 192, HALF), BF16),
            pltpu.VMEM((2, 4, 192, HALF), BF16),
            pltpu.VMEM((2, 4, 192, HALF), BF16),
            pltpu.VMEM((4, 48, CH), F32),
            pltpu.VMEM((4, 48, CH), BF16),
            pltpu.VMEM((4, 48, CH), BF16),
            pltpu.VMEM((3, 4, 8, CH), F32),
            dma((4,)),
            dma((1,)), dma((1,)),
            dma((2, 2)), dma((3, 2)), dma((2,)),
            dma((3, 2, 4)), dma((3, 2, 4)),
            dma((3, 2, 4)), dma((3, 2, 4)),
            dma((3, 2, 2, 4)), dma((3, 2, 2, 4)),
            dma((3, 2, 4)), dma((3, 2, 4)),
            dma((3, 2, 4)), dma((3, 2, 4)),
            dma((3,)), dma((3,)),
            dma((4,)), dma((4,)),
            dma((2, 3, 4)), dma((2, 3, 4)),
            dma((2, 3, 4)), dma((2, 3, 4)),
            dma((4,)), dma((4,)),
            dma((3, 4)), dma((3, 4)),
        ],
        compiler_params=pltpu.CompilerParams(
            collective_id=0, has_side_effects=True, vmem_limit_bytes=56 * 1024 * 1024
        ),
        cost_estimate=pl.CostEstimate(
            flops=2 * 256 * 256 * 3072 * 17, bytes_accessed=4 * 1024 * 1024, transcendentals=8 * 65536
        ),
    )(
        latents.reshape(CELLS, CH), cotangent.reshape(CELLS, CH), norm_gain, norm_shift,
        spatial_weight, temporal_weight,
    )
    spatial, temporal, norm = pl.pallas_call(
        unpack,
        out_shape=(
            jax.ShapeDtypeStruct((36, 1, CH), F32),
            jax.ShapeDtypeStruct((12, 1, CH), F32),
            jax.ShapeDtypeStruct((1, 2, CH), F32),
        ),
        in_specs=[vmem],
        out_specs=(vmem, vmem, vmem),
    )(packed)
    return (spatial.transpose(1, 0, 2), temporal.transpose(1, 0, 2), norm)


def solution(mesh):
    return jax.shard_map(
        shards,
        mesh=mesh,
        in_specs=(
            P("dp", None, None, None, None),
            P("dp", None, None, None, None),
            P("section", None, None),
            P("section", None, None),
            P("section", None),
            P("section", None),
        ),
        out_specs=(P("section", "dp", None), P("section", "dp", None), P("section", None, None)),
        check_vma=False,
    )
```
